128 devices in a mesh: row: 8 (over x_lo, z), col: 16 (over y, x_hi, core).
Axes of the slice: x: 4 (x_hi: 2, x_lo: 2; x = x_hi * 2 + x_lo), y: 4, z: 4, core: 2. Of those that a mesh axis runs over, the one named last changes fastest.
Arguments:
- grad_first: float32 [4096, 20480], P('row', 'col'), may hold values from -1000 to 1000
- grad_second: float32 [4096, 20480], P('row', 'col'), may hold values from -1000 to 1000
Outputs:
- update: float32 [4096, 20480], P('row', 'col')
The draws below stay inside these ranges and needn't reach their ends.
All inputs are finite; a program needn't handle non-finite values.
Results may differ from the reference program's by a relative error of at most 0.00014.
Values sent between devices are 32-bit elements; how exact they have to be, the bound alone decides.
No kernel may reach another device: no remote copies, remote signals or barrier semaphores. Data moves between devices by JAX's collectives and lax.ppermute only.
A program may use at most 128 MiB of HBM per device.

```python
import math
import jax
import jax.numpy as jnp
from jax import lax

D = 4096
FF = 20480
BLOCK = 256
ITERS = 6


def gradient_draw(key, step_number):
    own_key = jax.random.fold_in(key, 101 + step_number)
    row_key = jax.random.fold_in(key, 211)
    col_key = jax.random.fold_in(key, 223)
    upper_scale = 3.0
    entries = jax.random.normal(own_key, (D, FF), jnp.float32)
    row_scale = jnp.exp(jax.random.uniform(row_key, (D,), jnp.float32, 0.0, math.log(upper_scale)))
    col_scale = jnp.exp(jax.random.uniform(col_key, (FF,), jnp.float32, 0.0, math.log(upper_scale)))
    return entries * row_scale[:, None] * col_scale[None, :]


def draw_grad_first(key, part):
    return gradient_draw(key, 0)


def draw_grad_second(key, part):
    return gradient_draw(key, 1)


def setup_inputs(seed: int = 0) -> dict:
    streams_of = jax.random.split(jax.random.key(seed), 3)
    grad_first = draw_grad_first(jax.random.fold_in(streams_of[2], 71), 0)
    grad_second = draw_grad_second(jax.random.fold_in(streams_of[2], 71), 0)
    return dict(grad_first=grad_first, grad_second=grad_second)


damping = 0.001

def batched(left_mat, right_mat):
    return jnp.einsum('kij,kjl->kil', left_mat, right_mat, precision=lax.Precision.HIGHEST)

def newton_roots(statistic):
    width = statistic.shape[-1]
    identity = jnp.eye(width, dtype=jnp.float32)
    damped = statistic + damping * identity
    frob_norm = jnp.sqrt(lax.optimization_barrier(jnp.sum(damped * damped, axis=(1, 2))))
    scaled = damped / frob_norm[:, None, None]
    current = identity[None] * lax.rsqrt(jnp.sqrt(frob_norm))[:, None, None]
    for iteration in range(ITERS):
        factor = (5.0 * identity - scaled) / 4.0
        current = batched(current, factor)
        square = batched(factor, factor)
        scaled = batched(batched(square, square), scaled)
    return current

def reference(grad_first, grad_second):
    left_count = D // BLOCK
    right_count = FF // BLOCK
    left_state = jnp.zeros((left_count, BLOCK, BLOCK), jnp.float32)
    right_state = jnp.zeros((right_count, BLOCK, BLOCK), jnp.float32)
    update = jnp.zeros((D, FF), jnp.float32)
    for gradient in (grad_first, grad_second):
        row_blocks = gradient.reshape(left_count, BLOCK, FF)
        col_blocks = gradient.reshape(D, right_count, BLOCK)
        left_state = left_state + jnp.einsum('bik,bjk->bij', row_blocks, row_blocks, precision=lax.Precision.HIGHEST) / FF
        right_state = right_state + jnp.einsum('kbi,kbj->bij', col_blocks, col_blocks, precision=lax.Precision.HIGHEST) / D
        left_factor = newton_roots(left_state)
        right_factor = newton_roots(right_state)
        halfway = jnp.einsum('bij,bjk->bik', left_factor, row_blocks, precision=lax.Precision.HIGHEST).reshape(D, right_count, BLOCK)
        update = update + jnp.einsum('kbi,bij->kbj', halfway, right_factor, precision=lax.Precision.HIGHEST).reshape(D, FF)
    return update
```

```python
import functools

import jax
import jax.numpy as jnp
import numpy as np
from jax import lax
from jax.experimental import pallas as pl
from jax.experimental.pallas import tpu as pltpu
from jax.sharding import PartitionSpec as P

D = 4096
FF = 20480
BLOCK = 256
HALF = 128
ITERS = 6
DAMPING = 0.001
ROWS = 8
COLS = 16
RIGHT = 5
PACK = BLOCK + 8

f32 = jnp.float32
bf16 = jnp.bfloat16

OWNERS = ((0, 2, 1, 5, 7), (4, 6, 7, 1, 3))


def block_of(core, row):
    return OWNERS[core].index(row) if row in OWNERS[core] else -1


def order_table():
    table = np.zeros((2, ROWS, 2 * RIGHT), np.int32)
    for core in range(2):
        for row in range(ROWS):
            slots = [d for d in range(ROWS) if block_of(core, row ^ d) >= 0]
            table[core, row, :RIGHT] = slots
            table[core, row, RIGHT:] = [block_of(core, row ^ d) for d in slots]
    return table


def pairs_to_owners(d):
    return [
        (row * COLS + col, (row ^ d) * COLS + col)
        for row in range(ROWS)
        for col in range(COLS)
        if block_of(col % 2, row ^ d) >= 0
    ]


def pairs_from_owners(d):
    return [
        (row * COLS + col, (row ^ d) * COLS + col)
        for row in range(ROWS)
        for col in range(COLS)
        if block_of(col % 2, row) >= 0
    ]


def swap(value, d):
    return lax.ppermute(value, "col", [(i, i ^ d) for i in range(COLS)])


def parts(value):
    high = value.astype(bf16)
    return high, (value - high.astype(f32)).astype(bf16)


def dot(left, right, dims=((1,), (0,))):
    return lax.dot_general(left, right, (dims, ((), ())), preferred_element_type=f32)


def product(left, right, dims=((1,), (0,))):
    (lh, ll), (rh, rl) = left, right
    return dot(lh, rh, dims) + (dot(lh, rl, dims) + dot(ll, rh, dims))


def iotas(n):
    return (
        lax.broadcasted_iota(jnp.int32, (n, n), 0),
        lax.broadcasted_iota(jnp.int32, (n, n), 1),
    )


def store_packed(ref, start, block):
    i, j = iotas(HALF)
    first, last = block[:HALF, :HALF], block[HALF:, HALF:]
    ref[pl.ds(start, HALF), :] = block[:HALF, HALF:]
    ref[pl.ds(start + HALF, HALF), :] = jnp.where(i >= j, first, last)
    diagonal = jnp.sum(jnp.where(i == j, last, 0.0), axis=0, keepdims=True)
    ref[pl.ds(start + BLOCK, 8), :] = jnp.broadcast_to(diagonal, (8, HALF))


def unpacked(packed):
    i, j = iotas(HALF)
    upper, mixed, diagonal = packed[:HALF], packed[HALF:BLOCK], packed[BLOCK : BLOCK + 1]
    turned = mixed.T
    first = jnp.where(i >= j, mixed, turned)
    last = jnp.where(i < j, mixed, jnp.where(i == j, jnp.broadcast_to(diagonal, (HALF, HALF)), turned))
    return jnp.concatenate(
        [
            jnp.concatenate([first, upper], axis=1),
            jnp.concatenate([upper.T, last], axis=1),
        ],
        axis=0,
    )


def roots(statistics):
    i, j = iotas(BLOCK)
    identity = jnp.where(i == j, 1.0, 0.0).astype(f32)
    currents, scaleds = [], []
    for statistic in statistics:
        damped = statistic + DAMPING * identity
        norm = jnp.sqrt(jnp.sum(damped * damped, axis=(0, 1), keepdims=True))
        currents.append(lax.rsqrt(jnp.sqrt(norm)))
        scaleds.append(damped / norm)
    for iteration in range(ITERS):
        factors = [(5.0 * identity - scaled) * 0.25 for scaled in scaleds]
        split = [parts(factor) for factor in factors]
        if iteration == 0:
            currents = [current * factor for current, factor in zip(currents, factors)]
        else:
            currents = [product(parts(current), fs) for current, fs in zip(currents, split)]
        if iteration < ITERS - 1:
            squares = [parts(product(fs, fs)) for fs in split]
            fourths = [parts(product(sq, sq)) for sq in squares]
            scaleds = [product(fo, parts(scaled)) for fo, scaled in zip(fourths, scaleds)]
    return currents


def right_stats_kernel(table, first, second, *outs):
    step = pl.program_id(0)
    dims = ((0,), (0,))
    one = parts(first[...])
    two = parts(second[...])
    sum_one = product(one, one, dims) * (1.0 / D)
    sum_two = sum_one + product(two, two, dims) * (1.0 / D)
    for d in range(ROWS):

        @pl.when(table[step] == d)
        def _(d=d):
            store_packed(outs[d], 0, sum_one)
            store_packed(outs[d], PACK, sum_two)


def left_stats_kernel(info, first, second, keep, send):
    core = info[0]
    dims = ((1,), (1,))
    for out, block in ((keep, core), (send, 1 - core)):
        rows = pl.ds(pl.multiple_of(block * BLOCK, BLOCK), BLOCK)
        one = parts(first[rows, :])
        two = parts(second[rows, :])
        sum_one = product(one, one, dims) * (1.0 / FF)
        sum_two = sum_one + product(two, two, dims) * (1.0 / FF)
        store_packed(out, 0, sum_one)
        store_packed(out, PACK, sum_two)


def right_roots_kernel(*refs):
    ins, out = refs[:-1], refs[-1]
    total = ins[0][...]
    for ref in ins[1:]:
        total = total + ref[...]
    one, two = roots([unpacked(total[:PACK]), unpacked(total[PACK:])])
    store_packed(out, 0, one)
    store_packed(out, PACK, two)


def left_root_kernel(*refs):
    ins, out = refs[:-1], refs[-1]
    total = ins[0][...]
    for ref in ins[1:]:
        total = total + ref[...]
    (one,) = roots([unpacked(total)])
    store_packed(out, 0, one)


def halfway_kernel(info, first, second, mine, other, high_one, low_one, high_two, low_two, high, low):
    core = info[0]

    @pl.when(pl.program_id(0) == 0)
    def _():
        for b, ref in enumerate((mine, other)):
            for s in range(2):
                root = unpacked(ref[s * PACK : (s + 1) * PACK, :])
                high[2 * b + s], low[2 * b + s] = parts(root)

    for b, block in ((0, core), (1, 1 - core)):
        rows = pl.ds(pl.multiple_of(block * BLOCK, BLOCK), BLOCK)
        for s, source, high_out, low_out in ((0, first, high_one, low_one), (1, second, high_two, low_two)):
            result = product((high[2 * b + s], low[2 * b + s]), parts(source[rows, :]))
            high_out[rows, :], low_out[rows, :] = parts(result)


def apply_kernel(table, high_one, low_one, high_two, low_two, *refs):
    ins, out, held = refs[:ROWS], refs[ROWS], refs[ROWS + 1]
    step = pl.program_id(0)
    for d in range(ROWS):

        @pl.when(table[step] == d)
        def _(d=d):
            held[...] = ins[d][...]

    packed = held[...]
    one = parts(unpacked(packed[:PACK]))
    two = parts(unpacked(packed[PACK:]))
    out[...] = product((high_one[...], low_one[...]), one) + product((high_two[...], low_two[...]), two)


VMEM = pl.BlockSpec(memory_space=pltpu.VMEM)
SMEM = pl.BlockSpec(memory_space=pltpu.SMEM)


def params():
    return pltpu.CompilerParams(vmem_limit_bytes=40 * 1024 * 1024)


def cost(flops, moved):
    return pl.CostEstimate(flops=int(flops), bytes_accessed=int(moved), transcendentals=0)


def body(grad_first, grad_second):
    rows, cols = grad_first.shape
    row, col = lax.axis_index("row"), lax.axis_index("col")
    core = lax.rem(col, 2)
    high_x = lax.rem(col // 2, 2)
    table = jnp.asarray(order_table())[core, row]
    info = core.reshape(1).astype(jnp.int32)
    pair = jax.ShapeDtypeStruct((2 * PACK, HALF), f32)
    single = jax.ShapeDtypeStruct((PACK, HALF), f32)
    grads = 2 * rows * cols * 4
    passes = 3 * 2 * BLOCK * rows * cols * 2

    whole_pair = pl.BlockSpec((2 * PACK, HALF), lambda k, t: (0, 0))
    column = pl.BlockSpec((rows, BLOCK), lambda k, t: (0, t[RIGHT + k]))
    right_parts = pl.pallas_call(
        right_stats_kernel,
        grid_spec=pltpu.PrefetchScalarGridSpec(
            num_scalar_prefetch=1,
            grid=(RIGHT,),
            in_specs=[column, column],
            out_specs=[whole_pair] * ROWS,
        ),
        out_shape=[pair] * ROWS,
        compiler_params=params(),
        cost_estimate=cost(passes, grads),
        name="right_stats",
    )(table, grad_first, grad_second)
    arrived = [right_parts[0]] + [
        lax.ppermute(right_parts[d], ("row", "col"), pairs_to_owners(d)) for d in range(1, ROWS)
    ]

    keep, send = pl.pallas_call(
        left_stats_kernel,
        in_specs=[SMEM, VMEM, VMEM],
        out_specs=[VMEM, VMEM],
        out_shape=[pair, pair],
        compiler_params=params(),
        cost_estimate=cost(passes, grads),
        name="left_stats",
    )(info, grad_first, grad_second)
    both = (keep + swap(send, 1)).reshape(2, PACK, HALF)
    own = lax.dynamic_index_in_dim(both, high_x, 0, keepdims=False)
    own = own + swap(lax.dynamic_index_in_dim(both, 1 - high_x, 0, keepdims=False), 2)
    left_root = pl.pallas_call(
        left_root_kernel,
        in_specs=[VMEM] * 4,
        out_specs=VMEM,
        out_shape=single,
        compiler_params=params(),
        cost_estimate=cost(20 * 6 * BLOCK**3, 5 * PACK * HALF * 4),
        name="left_root",
    )(own, swap(own, 4), swap(own, 8), swap(own, 12))
    left_other = swap(left_root, 2)
    mine = jnp.where(
        high_x == 0,
        jnp.concatenate([left_root, left_other]),
        jnp.concatenate([left_other, left_root]),
    )
    other = swap(mine, 1)

    right_root = pl.pallas_call(
        right_roots_kernel,
        in_specs=[VMEM] * ROWS,
        out_specs=VMEM,
        out_shape=pair,
        compiler_params=params(),
        cost_estimate=cost(2 * 20 * 6 * BLOCK**3, 18 * PACK * HALF * 4),
        name="right_roots",
    )(*arrived)
    gathered = [right_root] + [
        lax.ppermute(right_root, ("row", "col"), pairs_from_owners(d)) for d in range(1, ROWS)
    ]

    halves = jax.ShapeDtypeStruct((rows, cols), bf16)
    tile = pl.BlockSpec((rows, BLOCK), lambda k: (0, k))
    halfway = pl.pallas_call(
        halfway_kernel,
        grid=(RIGHT,),
        in_specs=[SMEM, tile, tile, VMEM, VMEM],
        out_specs=[tile] * 4,
        out_shape=[halves] * 4,
        scratch_shapes=[pltpu.VMEM((4, BLOCK, BLOCK), bf16), pltpu.VMEM((4, BLOCK, BLOCK), bf16)],
        compiler_params=params(),
        cost_estimate=cost(passes, 2 * grads),
        name="halfway",
    )(info, grad_first, grad_second, mine, other)

    return pl.pallas_call(
        apply_kernel,
        grid_spec=pltpu.PrefetchScalarGridSpec(
            num_scalar_prefetch=1,
            grid=(RIGHT,),
            in_specs=[column] * 4 + [whole_pair] * ROWS,
            out_specs=column,
            scratch_shapes=[pltpu.VMEM((2 * PACK, HALF), f32)],
        ),
        out_shape=jax.ShapeDtypeStruct((rows, cols), f32),
        compiler_params=params(),
        cost_estimate=cost(passes, 2 * grads),
        name="apply",
    )(table, *halfway, *gathered)


def solution(mesh):
    in_specs = (P("row", "col"), P("row", "col"))
    out_specs = P("row", "col")
    return jax.shard_map(body, mesh=mesh, in_specs=in_specs, out_specs=out_specs, check_vma=False)
```

```python
import jax
import jax.numpy as jnp
from jax import lax
from jax.experimental import pallas as pl
from jax.experimental.pallas import tpu as pltpu
from jax.sharding import PartitionSpec as P

D = 4096
FF = 20480
BLOCK = 256
HALF = 128
ITERS = 6
DAMPING = 0.001
ROWS = 8
COLS = 16
RIGHT = 5
SHARE = 2 * BLOCK // ROWS
SLOT = BLOCK + 8 + SHARE
EXTRA = 8 + SHARE
PACK = BLOCK + 8

f32 = jnp.float32
bf16 = jnp.bfloat16

def swap(value, d):
    return lax.ppermute(value, "col", [(i, i ^ d) for i in range(COLS)])


def exchanged(slots):
    return lax.all_to_all(slots, "row", split_axis=0, concat_axis=0, tiled=True)


def parts(value):
    high = value.astype(bf16)
    return high, (value - high.astype(f32)).astype(bf16)


def dot(left, right, dims=((1,), (0,))):
    return lax.dot_general(left, right, (dims, ((), ())), preferred_element_type=f32)


def product(left, right, dims=((1,), (0,))):
    (lh, ll), (rh, rl) = left, right
    return dot(lh, rh, dims) + (dot(lh, rl, dims) + dot(ll, rh, dims))


def iotas(n):
    return (
        lax.broadcasted_iota(jnp.int32, (n, n), 0),
        lax.broadcasted_iota(jnp.int32, (n, n), 1),
    )


def packed_parts(block):
    i, j = iotas(HALF)
    first, last = block[:HALF, :HALF], block[HALF:, HALF:]
    quarters = jnp.concatenate([block[:HALF, HALF:], jnp.where(i >= j, first, last)], axis=0)
    return quarters, jnp.sum(jnp.where(i == j, last, 0.0), axis=0, keepdims=True)


def packed_gram(even, odd):
    i, j = iotas(HALF)
    first, last = odd[:HALF, :HALF], odd[HALF:, HALF:]
    upper = even[:HALF, HALF:] + odd[:HALF, HALF:] + odd[HALF:, :HALF].T
    mixed = jnp.where(i >= j, even[:HALF, :HALF] + first, even[HALF:, HALF:] + last)
    mixed = mixed + jnp.where(i <= j, first, last).T
    diagonal = jnp.sum(jnp.where(i == j, even[HALF:, HALF:] + 2.0 * last, 0.0), axis=0, keepdims=True)
    return jnp.concatenate([upper, mixed], axis=0), diagonal


def store_packed(ref, start, block):
    quarters, diagonal = packed_parts(block)
    ref[pl.ds(start, BLOCK), :] = quarters
    ref[pl.ds(start + BLOCK, 8), :] = jnp.broadcast_to(diagonal, (8, HALF))


def unpacked(packed, diagonal=None):
    i, j = iotas(HALF)
    upper, mixed = packed[:HALF], packed[HALF:BLOCK]
    if diagonal is None:
        diagonal = packed[BLOCK : BLOCK + 1]
    turned = mixed.T
    first = jnp.where(i >= j, mixed, turned)
    last = jnp.where(i < j, mixed, jnp.where(i == j, jnp.broadcast_to(diagonal, (HALF, HALF)), turned))
    return jnp.concatenate(
        [
            jnp.concatenate([first, upper], axis=1),
            jnp.concatenate([upper.T, last], axis=1),
        ],
        axis=0,
    )


def roots(statistics):
    i, j = iotas(BLOCK)
    identity = jnp.where(i == j, 1.0, 0.0).astype(f32)
    currents, scaleds = [], []
    for statistic in statistics:
        damped = statistic + DAMPING * identity
        norm = jnp.sqrt(jnp.sum(damped * damped, axis=(0, 1), keepdims=True))
        currents.append(lax.rsqrt(jnp.sqrt(norm)))
        scaleds.append(damped / norm)
    for iteration in range(ITERS):
        factors = [(5.0 * identity - scaled) * 0.25 for scaled in scaleds]
        split = [parts(factor) for factor in factors]
        if iteration == 0:
            currents = [current * factor for current, factor in zip(currents, factors)]
        else:
            currents = [product(parts(current), fs) for current, fs in zip(currents, split)]
        if iteration < ITERS - 1:
            squares = [parts(product(fs, fs)) for fs in split]
            fourths = [parts(product(sq, sq)) for sq in squares]
            scaleds = [product(fo, parts(scaled)) for fo, scaled in zip(fourths, scaleds)]
    return currents


def fetched(sources, buffer, sems):
    tiles = []
    for b in range(RIGHT):
        columns = pl.ds(b * BLOCK, BLOCK)
        tiles.append(
            [
                pltpu.make_async_copy(source.at[:, columns], buffer.at[s, b], sems.at[s, b])
                for s, source in enumerate(sources)
            ]
        )
    for copies in tiles:
        for copy in copies:
            copy.start()
    return tiles


def right_stats_kernel(first, second, out, buffer, sems):
    tiles = fetched((first, second), buffer, sems)
    half = ROWS // 2
    for b in range(RIGHT):
        total = None
        for s in range(2):
            tiles[b][s].wait()
            high, low = parts(buffer[s, b])
            gram = dot(high, jnp.concatenate([high, low], axis=1), ((0,), (0,))) * (1.0 / D)
            gram = packed_gram(gram[:, :BLOCK], gram[:, BLOCK:])
            total = gram if s == 0 else (total[0] + gram[0], total[1] + gram[1])
            if b < RIGHT - 1:
                out[2 * b + s, :BLOCK, :] = total[0]
                out[2 * b + s, BLOCK : BLOCK + 1, :] = total[1]
            else:
                out[s * half : (s + 1) * half, BLOCK + 8 :, :] = total[0].reshape(half, SHARE, HALF)
                for slot in range(ROWS):
                    out[slot, BLOCK + 1 + s : BLOCK + 2 + s, :] = total[1]
    for slot in range(ROWS):
        out[slot, BLOCK + 3 : BLOCK + 8, :] = jnp.zeros((5, HALF), f32)


def left_stats_kernel(info, first, second, keep, send, buffer, sums, sems):
    core = info[0]
    tiles = fetched((first, second), buffer, sems)
    for b in range(RIGHT):
        for s in range(2):
            tiles[b][s].wait()
            for block in range(2):
                high, low = parts(buffer[s, b, block * BLOCK : (block + 1) * BLOCK, :])
                gram = dot(high, jnp.concatenate([high, low], axis=0), ((1,), (1,)))
                if b == 0:
                    sums[block, s] = gram
                else:
                    sums[block, s] += gram
    for out, block in ((keep, core), (send, 1 - core)):
        total = None
        for s in range(2):
            gram = sums[block, s] * (1.0 / FF)
            gram = packed_gram(gram[:, :BLOCK], gram[:, BLOCK:])
            total = gram if s == 0 else (total[0] + gram[0], total[1] + gram[1])
            out[s * PACK : s * PACK + BLOCK, :] = total[0]
            out[s * PACK + BLOCK : (s + 1) * PACK, :] = jnp.broadcast_to(total[1], (8, HALF))


def share_kernel(arrived, out, buffer, sem):
    copy = pltpu.make_async_copy(arrived.at[:, pl.ds(BLOCK, EXTRA), :], buffer, sem)
    copy.start()
    copy.wait()
    total = buffer[0]
    for slot in range(1, ROWS):
        total = total + buffer[slot]
    for slot in range(ROWS):
        out[slot] = total


def roots_kernel(arrived, left_own, left_other, right_out, left_out, buffer, sems):
    copies = [
        pltpu.make_async_copy(arrived.at[slot, pl.ds(0, PACK), :], buffer.at[slot], sems.at[slot])
        for slot in range(ROWS)
    ]
    for copy in copies:
        copy.start()
    left_total = left_own[...] + left_other[...]
    copies[0].wait()
    total = buffer[0]
    for slot in range(1, ROWS):
        copies[slot].wait()
        total = total + buffer[slot]
    right_root, left_root = roots([unpacked(total), unpacked(left_total)])
    quarters, diagonal = packed_parts(right_root)
    for slot in range(ROWS):
        right_out[slot, :BLOCK, :] = quarters
        right_out[slot, BLOCK:, :] = jnp.broadcast_to(diagonal, (8, HALF))
    store_packed(left_out, 0, left_root)


def shared_roots_kernel(gathered, out):
    half = ROWS // 2
    statistics = [
        unpacked(
            gathered[s * half : (s + 1) * half, 8:, :].reshape(BLOCK, HALF), gathered[0, 1 + s : 2 + s, :]
        )
        for s in range(2)
    ]
    for s, root in enumerate(roots(statistics)):
        out[s] = root


def halfway_kernel(info, first, second, mine, other, out, buffer, results, sems, out_sems):
    core = info[0]
    tiles = fetched((first, second), buffer, sems)
    split = [[parts(unpacked(ref[s * PACK : (s + 1) * PACK, :])) for s in range(2)] for ref in (mine, other)]
    copies = []
    for b in range(RIGHT):
        for s in range(2):
            tiles[b][s].wait()
            for place, block in enumerate((core, 1 - core)):
                rows = pl.ds(pl.multiple_of(block * BLOCK, BLOCK), BLOCK)
                result = product(split[place][s], parts(buffer[s, b, rows, :]))
                results[b, 2 * s, rows, :], results[b, 2 * s + 1, rows, :] = parts(result)
        copy = pltpu.make_async_copy(results.at[b], out.at[b], out_sems.at[b])
        copy.start()
        copies.append(copy)
    for copy in copies:
        copy.wait()


def apply_kernel(halfway, gathered, shared, out, held, roots_in, buffer, sems, root_sems, out_sems):
    order = (RIGHT - 1, *range(RIGHT - 1))
    fetches = []
    for b in order:
        fetches.append([pltpu.make_async_copy(halfway.at[b], held.at[b], sems.at[b])])
        if b < RIGHT - 1:
            fetches[-1].append(
                pltpu.make_async_copy(gathered.at[pl.ds(2 * b, 2)], roots_in.at[pl.ds(2 * b, 2)], root_sems.at[b])
            )
        for copy in fetches[-1]:
            copy.start()
    copies = []
    for b, fetch in zip(order, fetches):
        for copy in fetch:
            copy.wait()
        if b == RIGHT - 1:
            one, two = parts(shared[0]), parts(shared[1])
        else:
            one, two = parts(unpacked(roots_in[2 * b])), parts(unpacked(roots_in[2 * b + 1]))
        buffer[b] = product((held[b, 0], held[b, 1]), one) + product((held[b, 2], held[b, 3]), two)
        copy = pltpu.make_async_copy(buffer.at[b], out.at[:, pl.ds(b * BLOCK, BLOCK)], out_sems.at[b])
        copy.start()
        copies.append(copy)
    for copy in copies:
        copy.wait()


VMEM = pl.BlockSpec(memory_space=pltpu.VMEM)
SMEM = pl.BlockSpec(memory_space=pltpu.SMEM)
HBM = pl.BlockSpec(memory_space=pltpu.HBM)
ANY = pl.BlockSpec(memory_space=pl.ANY)


def in_hbm(*values):
    return [pltpu.with_memory_space_constraint(value, pltpu.HBM) for value in values]


def params():
    return pltpu.CompilerParams(vmem_limit_bytes=32 * 1024 * 1024)


def cost(flops, moved):
    return pl.CostEstimate(flops=int(flops), bytes_accessed=int(moved), transcendentals=0)


def body(grad_first, grad_second):
    rows, cols = grad_first.shape
    col = lax.axis_index("col")
    core = lax.rem(col, 2)
    low_y = lax.rem(col // 4, 2)
    info = core.reshape(1).astype(jnp.int32)
    pair = jax.ShapeDtypeStruct((2 * PACK, HALF), f32)
    single = jax.ShapeDtypeStruct((PACK, HALF), f32)
    grads = 2 * rows * cols * 4
    passes = 3 * 2 * BLOCK * rows * cols * 2
    newton = 20 * 6 * BLOCK**3
    tiles = [pltpu.VMEM((2, RIGHT, rows, BLOCK), f32)]
    tile_sems = [pltpu.SemaphoreType.DMA((2, RIGHT))]

    right_parts = pl.pallas_call(
        right_stats_kernel,
        in_specs=[HBM, HBM],
        out_specs=VMEM,
        out_shape=jax.ShapeDtypeStruct((ROWS, SLOT, HALF), f32),
        scratch_shapes=tiles + tile_sems,
        compiler_params=params(),
        cost_estimate=cost(passes, grads),
        name="right_stats",
    )(*in_hbm(grad_first, grad_second))
    arrived = exchanged(right_parts)

    info, right_parts = lax.optimization_barrier((info, right_parts))
    keep, send = pl.pallas_call(
        left_stats_kernel,
        in_specs=[SMEM, HBM, HBM],
        out_specs=[VMEM, VMEM],
        out_shape=[pair, pair],
        scratch_shapes=tiles + [pltpu.VMEM((2, 2, BLOCK, 2 * BLOCK), f32)] + tile_sems,
        compiler_params=params(),
        cost_estimate=cost(passes, grads),
        name="left_stats",
    )(info, *in_hbm(grad_first, grad_second))
    both = (keep + swap(send, 1)).reshape(2, PACK, HALF)
    own = lax.dynamic_index_in_dim(both, low_y, 0, keepdims=False)
    rest = lax.dynamic_index_in_dim(both, 1 - low_y, 0, keepdims=False)
    own = (own + swap(rest, 4)) + (swap(own, 8) + swap(rest, 12))
    left_in = [own, swap(own, 2)]

    shares = exchanged(
        pl.pallas_call(
            share_kernel,
            in_specs=[ANY],
            out_specs=VMEM,
            out_shape=jax.ShapeDtypeStruct((ROWS, EXTRA, HALF), f32),
            scratch_shapes=[pltpu.VMEM((ROWS, EXTRA, HALF), f32), pltpu.SemaphoreType.DMA(())],
            compiler_params=params(),
            cost_estimate=cost(0, 2 * ROWS * EXTRA * HALF * 4),
            name="share",
        )(arrived)
    )
    right_root, left_root = pl.pallas_call(
        roots_kernel,
        in_specs=[ANY] + [VMEM] * 2,
        out_specs=[VMEM, VMEM],
        out_shape=[jax.ShapeDtypeStruct((ROWS, PACK, HALF), f32), single],
        scratch_shapes=[pltpu.VMEM((ROWS, PACK, HALF), f32), pltpu.SemaphoreType.DMA((ROWS,))],
        compiler_params=params(),
        cost_estimate=cost(2 * newton, 2 * ROWS * PACK * HALF * 4),
        name="roots",
    )(arrived, *left_in)
    gathered = exchanged(right_root)

    left_other = swap(left_root, 4)
    mine = jnp.where(
        low_y == 0,
        jnp.concatenate([left_root, left_other]),
        jnp.concatenate([left_other, left_root]),
    )
    other = swap(mine, 1)
    shared = pl.pallas_call(
        shared_roots_kernel,
        in_specs=[VMEM],
        out_specs=VMEM,
        out_shape=jax.ShapeDtypeStruct((2, BLOCK, BLOCK), f32),
        compiler_params=params(),
        cost_estimate=cost(2 * newton, 4 * PACK * HALF * 4),
        name="shared_roots",
    )(shares)

    held = (RIGHT, 4, rows, BLOCK)
    tile_sem = pltpu.SemaphoreType.DMA((RIGHT,))
    halfway = pl.pallas_call(
        halfway_kernel,
        in_specs=[SMEM, HBM, HBM, VMEM, VMEM],
        out_specs=HBM,
        out_shape=pltpu.HBM(held, bf16),
        scratch_shapes=tiles + [pltpu.VMEM(held, bf16)] + tile_sems + [tile_sem],
        compiler_params=params(),
        cost_estimate=cost(passes, 2 * grads),
        name="halfway",
    )(info, *in_hbm(grad_first, grad_second), mine, other)

    return pl.pallas_call(
        apply_kernel,
        in_specs=[HBM, ANY, VMEM],
        out_specs=HBM,
        scratch_shapes=[
            pltpu.VMEM(held, bf16),
            pltpu.VMEM((ROWS, PACK, HALF), f32),
            pltpu.VMEM((RIGHT, rows, BLOCK), f32),
            tile_sem,
            tile_sem,
            tile_sem,
        ],
        out_shape=jax.ShapeDtypeStruct((rows, cols), f32),
        compiler_params=params(),
        cost_estimate=cost(passes, 2 * grads),
        name="apply",
    )(*in_hbm(halfway), gathered, shared)


def solution(mesh):
    in_specs = (P("row", "col"), P("row", "col"))
    out_specs = P("row", "col")
    return jax.shard_map(body, mesh=mesh, in_specs=in_specs, out_specs=out_specs, check_vma=False)
```

```python
import jax
import jax.numpy as jnp
from jax import lax
from jax.experimental import pallas as pl
from jax.experimental.pallas import tpu as pltpu
from jax.sharding import PartitionSpec as P

D = 4096
FF = 20480
BLOCK = 256
HALF = 128
ITERS = 6
DAMPING = 0.001
ROWS = 8
COLS = 16
RIGHT = 5
SHARE = 2 * BLOCK // ROWS
SLOT = BLOCK + 8 + SHARE
PACK = BLOCK + 8

f32 = jnp.float32
bf16 = jnp.bfloat16

def swap(value, d):
    return lax.ppermute(value, "col", [(i, i ^ d) for i in range(COLS)])


def exchanged(slots):
    return lax.all_to_all(slots, "row", split_axis=0, concat_axis=0, tiled=True)


def parts(value):
    high = value.astype(bf16)
    return high, (value - high.astype(f32)).astype(bf16)


def dot(left, right, dims=((1,), (0,))):
    return lax.dot_general(left, right, (dims, ((), ())), preferred_element_type=f32)


def product(left, right, dims=((1,), (0,))):
    (lh, ll), (rh, rl) = left, right
    return dot(lh, rh, dims) + (dot(lh, rl, dims) + dot(ll, rh, dims))


def iotas(n):
    return (
        lax.broadcasted_iota(jnp.int32, (n, n), 0),
        lax.broadcasted_iota(jnp.int32, (n, n), 1),
    )


def packed_parts(block):
    i, j = iotas(HALF)
    first, last = block[:HALF, :HALF], block[HALF:, HALF:]
    quarters = jnp.concatenate([block[:HALF, HALF:], jnp.where(i >= j, first, last)], axis=0)
    return quarters, jnp.sum(jnp.where(i == j, last, 0.0), axis=0, keepdims=True)


def packed_gram(even, odd):
    i, j = iotas(HALF)
    first, last = odd[:HALF, :HALF], odd[HALF:, HALF:]
    upper = even[:HALF, HALF:] + odd[:HALF, HALF:] + odd[HALF:, :HALF].T
    mixed = jnp.where(i >= j, even[:HALF, :HALF] + first, even[HALF:, HALF:] + last)
    mixed = mixed + jnp.where(i <= j, first, last).T
    diagonal = jnp.sum(jnp.where(i == j, even[HALF:, HALF:] + 2.0 * last, 0.0), axis=0, keepdims=True)
    return jnp.concatenate([upper, mixed], axis=0), diagonal


def store_packed(ref, start, block):
    quarters, diagonal = packed_parts(block)
    ref[pl.ds(start, BLOCK), :] = quarters
    ref[pl.ds(start + BLOCK, 8), :] = jnp.broadcast_to(diagonal, (8, HALF))


def unpacked(packed, diagonal=None):
    i, j = iotas(HALF)
    upper, mixed = packed[:HALF], packed[HALF:BLOCK]
    if diagonal is None:
        diagonal = packed[BLOCK : BLOCK + 1]
    turned = mixed.T
    first = jnp.where(i >= j, mixed, turned)
    last = jnp.where(i < j, mixed, jnp.where(i == j, jnp.broadcast_to(diagonal, (HALF, HALF)), turned))
    return jnp.concatenate(
        [
            jnp.concatenate([first, upper], axis=1),
            jnp.concatenate([upper.T, last], axis=1),
        ],
        axis=0,
    )


def root_steps(statistics, found):
    i, j = iotas(BLOCK)
    identity = jnp.where(i == j, 1.0, 0.0).astype(f32)
    currents, scaleds = [], []
    for statistic in statistics:
        damped = statistic + DAMPING * identity
        norm = jnp.sqrt(jnp.sum(damped * damped, axis=(0, 1), keepdims=True))
        currents.append(lax.rsqrt(jnp.sqrt(norm)))
        scaleds.append(damped / norm)
    for iteration in range(ITERS):
        factors = [(5.0 * identity - scaled) * 0.25 for scaled in scaleds]
        split = [parts(factor) for factor in factors]
        if iteration == ITERS - 1:
            found.extend(product(parts(current), fs) for current, fs in zip(currents, split))
            return
        squares = [parts(product(fs, fs)) for fs in split]
        yield
        if iteration == 0:
            currents = [current * factor for current, factor in zip(currents, factors)]
        else:
            currents = [product(parts(current), fs) for current, fs in zip(currents, split)]
        fourths = [parts(product(sq, sq)) for sq in squares]
        yield
        scaleds = [product(fo, parts(scaled)) for fo, scaled in zip(fourths, scaleds)]
        yield


def roots(statistics):
    found = []
    for _ in root_steps(statistics, found):
        pass
    return found


def fetched(sources, buffer, sems):
    tiles = []
    for b in range(RIGHT):
        columns = pl.ds(b * BLOCK, BLOCK)
        tiles.append(
            [
                pltpu.make_async_copy(source.at[:, columns], buffer.at[s, b], sems.at[s, b])
                for s, source in enumerate(sources)
            ]
        )
    for copies in tiles:
        for copy in copies:
            copy.start()
    return tiles


def right_stats_kernel(first, second, out, buffer, sems):
    tiles = fetched((first, second), buffer, sems)
    half = ROWS // 2
    for b in range(RIGHT):
        total = None
        for s in range(2):
            tiles[b][s].wait()
            high, low = parts(buffer[s, b])
            gram = dot(high, jnp.concatenate([high, low], axis=1), ((0,), (0,))) * (1.0 / D)
            gram = packed_gram(gram[:, :BLOCK], gram[:, BLOCK:])
            total = gram if s == 0 else (total[0] + gram[0], total[1] + gram[1])
            if b < RIGHT - 1:
                out[2 * b + s, :BLOCK, :] = total[0]
                out[2 * b + s, BLOCK : BLOCK + 1, :] = total[1]
            else:
                out[s * half : (s + 1) * half, BLOCK + 8 :, :] = total[0].reshape(half, SHARE, HALF)
                for slot in range(ROWS):
                    out[slot, BLOCK + 1 + s : BLOCK + 2 + s, :] = total[1]
    for slot in range(ROWS):
        out[slot, BLOCK + 3 : BLOCK + 8, :] = jnp.zeros((5, HALF), f32)


def left_stats_kernel(info, first, second, keep, send, buffer, sums, sems):
    core = info[0]
    tiles = fetched((first, second), buffer, sems)
    for b in range(RIGHT):
        for s in range(2):
            tiles[b][s].wait()
            for block in range(2):
                high, low = parts(buffer[s, b, block * BLOCK : (block + 1) * BLOCK, :])
                gram = dot(high, jnp.concatenate([high, low], axis=0), ((1,), (1,)))
                if b == 0:
                    sums[block, s] = gram
                else:
                    sums[block, s] += gram
    for out, block in ((keep, core), (send, 1 - core)):
        total = None
        for s in range(2):
            gram = sums[block, s] * (1.0 / FF)
            gram = packed_gram(gram[:, :BLOCK], gram[:, BLOCK:])
            total = gram if s == 0 else (total[0] + gram[0], total[1] + gram[1])
            out[s * PACK : s * PACK + BLOCK, :] = total[0]
            out[s * PACK + BLOCK : (s + 1) * PACK, :] = jnp.broadcast_to(total[1], (8, HALF))


def right_roots_kernel(arrived, right_out, diagonals, buffer, sems):
    copies = [pltpu.make_async_copy(arrived.at[slot], buffer.at[slot], sems.at[slot]) for slot in range(ROWS)]
    for copy in copies:
        copy.start()
    copies[0].wait()
    total = buffer[0]
    for slot in range(1, ROWS):
        copies[slot].wait()
        total = total + buffer[slot]
    for slot in range(ROWS):
        right_out[slot, PACK:, :] = total[PACK:]
    diagonals[...] = total[BLOCK:PACK]
    (root,) = roots([unpacked(total[:PACK])])
    quarters, diagonal = packed_parts(root)
    for slot in range(ROWS):
        right_out[slot, :BLOCK, :] = quarters
        right_out[slot, BLOCK:PACK, :] = jnp.broadcast_to(diagonal, (8, HALF))


def left_root_kernel(own, other, out):
    (root,) = roots([unpacked(own[...] + other[...])])
    store_packed(out, 0, root)


def halfway_kernel(info, first, second, mine, other, out, buffer, results, sems, out_sems):
    core = info[0]
    tiles = fetched((first, second), buffer, sems)
    split = [[parts(unpacked(ref[s * PACK : (s + 1) * PACK, :])) for s in range(2)] for ref in (mine, other)]
    copies = []
    for b in range(RIGHT):
        for s in range(2):
            tiles[b][s].wait()
            for place, block in enumerate((core, 1 - core)):
                rows = pl.ds(pl.multiple_of(block * BLOCK, BLOCK), BLOCK)
                result = product(split[place][s], parts(buffer[s, b, rows, :]))
                results[b, 2 * s, rows, :], results[b, 2 * s + 1, rows, :] = parts(result)
        copy = pltpu.make_async_copy(results.at[b], out.at[b], out_sems.at[b])
        copy.start()
        copies.append(copy)
    for copy in copies:
        copy.wait()


def applied(held, b, one, two, buffer):
    (h1, l1), (h2, l2) = one, two
    weights = jnp.concatenate([h1, h1, l1, h2, h2, l2], axis=0)
    for start in (0, BLOCK):
        rows = slice(start, start + BLOCK)
        high_one, low_one, high_two, low_two = [held[b, q, rows, :] for q in range(4)]
        lhs = jnp.concatenate([low_one, high_one, high_one, low_two, high_two, high_two], axis=1)
        buffer[b, rows, :] = dot(lhs, weights)
        yield


def finish_kernel(
    halfway, gathered, diagonals, out, held, roots_in, shares, buffer, sems, root_sems, share_sem, out_sems
):
    share_copy = pltpu.make_async_copy(gathered.at[:, pl.ds(PACK, SHARE), :], shares, share_sem)
    share_copy.start()
    fetches = []
    for b in range(RIGHT):
        fetches.append([])
        if b < RIGHT - 1:
            pair = pl.ds(2 * b, 2)
            fetches[b].append(
                pltpu.make_async_copy(
                    gathered.at[pair, pl.ds(0, PACK), :], roots_in.at[pair], root_sems.at[b]
                )
            )
        fetches[b].append(pltpu.make_async_copy(halfway.at[b], held.at[b], sems.at[b]))
        for copy in fetches[b]:
            copy.start()
    half = ROWS // 2
    share_copy.wait()
    statistics = [
        unpacked(shares[s * half : (s + 1) * half].reshape(BLOCK, HALF), diagonals[1 + s : 2 + s, :])
        for s in range(2)
    ]
    found = []
    chain = root_steps(statistics, found)
    copies = []

    def stored(b):
        copy = pltpu.make_async_copy(buffer.at[b], out.at[:, pl.ds(b * BLOCK, BLOCK)], out_sems.at[b])
        copy.start()
        copies.append(copy)

    next(chain)
    for b in range(RIGHT - 1):
        for copy in fetches[b]:
            copy.wait()
        one, two = parts(unpacked(roots_in[2 * b])), parts(unpacked(roots_in[2 * b + 1]))
        for _ in applied(held, b, one, two, buffer):
            next(chain, None)
        stored(b)
        next(chain, None)
    for _ in chain:
        pass
    last = RIGHT - 1
    fetches[last][0].wait()
    for _ in applied(held, last, parts(found[0]), parts(found[1]), buffer):
        pass
    stored(last)
    for copy in copies:
        copy.wait()


VMEM = pl.BlockSpec(memory_space=pltpu.VMEM)
SMEM = pl.BlockSpec(memory_space=pltpu.SMEM)
HBM = pl.BlockSpec(memory_space=pltpu.HBM)
ANY = pl.BlockSpec(memory_space=pl.ANY)


def in_hbm(*values):
    return [pltpu.with_memory_space_constraint(value, pltpu.HBM) for value in values]


def params():
    return pltpu.CompilerParams(vmem_limit_bytes=32 * 1024 * 1024)


def cost(flops, moved):
    return pl.CostEstimate(flops=int(flops), bytes_accessed=int(moved), transcendentals=0)


def body(grad_first, grad_second):
    rows, cols = grad_first.shape
    col = lax.axis_index("col")
    core = lax.rem(col, 2)
    low_y = lax.rem(col // 4, 2)
    info = core.reshape(1).astype(jnp.int32)
    pair = jax.ShapeDtypeStruct((2 * PACK, HALF), f32)
    single = jax.ShapeDtypeStruct((PACK, HALF), f32)
    grads = 2 * rows * cols * 4
    passes = 3 * 2 * BLOCK * rows * cols * 2
    newton = 20 * 6 * BLOCK**3
    tiles = [pltpu.VMEM((2, RIGHT, rows, BLOCK), f32)]
    tile_sems = [pltpu.SemaphoreType.DMA((2, RIGHT))]

    right_parts = pl.pallas_call(
        right_stats_kernel,
        in_specs=[HBM, HBM],
        out_specs=VMEM,
        out_shape=jax.ShapeDtypeStruct((ROWS, SLOT, HALF), f32),
        scratch_shapes=tiles + tile_sems,
        compiler_params=params(),
        cost_estimate=cost(passes, grads),
        name="right_stats",
    )(*in_hbm(grad_first, grad_second))
    arrived = exchanged(right_parts)

    info, right_parts = lax.optimization_barrier((info, right_parts))
    keep, send = pl.pallas_call(
        left_stats_kernel,
        in_specs=[SMEM, HBM, HBM],
        out_specs=[VMEM, VMEM],
        out_shape=[pair, pair],
        scratch_shapes=tiles + [pltpu.VMEM((2, 2, BLOCK, 2 * BLOCK), f32)] + tile_sems,
        compiler_params=params(),
        cost_estimate=cost(passes, grads),
        name="left_stats",
    )(info, *in_hbm(grad_first, grad_second))
    both = (keep + swap(send, 1)).reshape(2, PACK, HALF)
    own = lax.dynamic_index_in_dim(both, low_y, 0, keepdims=False)
    rest = lax.dynamic_index_in_dim(both, 1 - low_y, 0, keepdims=False)
    own = (own + swap(rest, 4)) + (swap(own, 8) + swap(rest, 12))
    own, arrived = lax.optimization_barrier((own, arrived))
    left_in = [own, swap(own, 2)]

    slots = jax.ShapeDtypeStruct((ROWS, SLOT, HALF), f32)
    right_root, diagonals = pl.pallas_call(
        right_roots_kernel,
        in_specs=[ANY],
        out_specs=[VMEM, VMEM],
        out_shape=[slots, jax.ShapeDtypeStruct((8, HALF), f32)],
        scratch_shapes=[pltpu.VMEM((ROWS, SLOT, HALF), f32), pltpu.SemaphoreType.DMA((ROWS,))],
        compiler_params=params(),
        cost_estimate=cost(newton, 2 * ROWS * SLOT * HALF * 4),
        name="right_roots",
    )(arrived)
    left_in, right_root = lax.optimization_barrier((left_in, right_root))
    gathered = exchanged(right_root)
    left_in, right_root = lax.optimization_barrier((left_in, right_root))
    left_root = pl.pallas_call(
        left_root_kernel,
        in_specs=[VMEM, VMEM],
        out_specs=VMEM,
        out_shape=single,
        compiler_params=params(),
        cost_estimate=cost(newton, 3 * PACK * HALF * 4),
        name="left_root",
    )(*left_in)
    left_other = swap(left_root, 4)
    mine = jnp.where(
        low_y == 0,
        jnp.concatenate([left_root, left_other]),
        jnp.concatenate([left_other, left_root]),
    )
    other = swap(mine, 1)

    held = (RIGHT, 4, rows, BLOCK)
    tile_sem = pltpu.SemaphoreType.DMA((RIGHT,))
    halfway = pl.pallas_call(
        halfway_kernel,
        in_specs=[SMEM, HBM, HBM, VMEM, VMEM],
        out_specs=HBM,
        out_shape=pltpu.HBM(held, bf16),
        scratch_shapes=tiles + [pltpu.VMEM(held, bf16)] + tile_sems + [tile_sem],
        compiler_params=params(),
        cost_estimate=cost(passes, 2 * grads),
        name="halfway",
    )(info, *in_hbm(grad_first, grad_second), mine, other)

    return pl.pallas_call(
        finish_kernel,
        in_specs=[HBM, ANY, VMEM],
        out_specs=HBM,
        scratch_shapes=[
            pltpu.VMEM(held, bf16),
            pltpu.VMEM((ROWS, PACK, HALF), f32),
            pltpu.VMEM((ROWS, SHARE, HALF), f32),
            pltpu.VMEM((RIGHT, rows, BLOCK), f32),
            tile_sem,
            tile_sem,
            pltpu.SemaphoreType.DMA(()),
            tile_sem,
        ],
        out_shape=jax.ShapeDtypeStruct((rows, cols), f32),
        compiler_params=params(),
        cost_estimate=cost(passes + 2 * newton, 2 * grads),
        name="finish",
    )(*in_hbm(halfway), gathered, diagonals)


def solution(mesh):
    in_specs = (P("row", "col"), P("row", "col"))
    out_specs = P("row", "col")
    return jax.shard_map(body, mesh=mesh, in_specs=in_specs, out_specs=out_specs, check_vma=False)
```

```python
import jax
import jax.numpy as jnp
from jax import lax
from jax.experimental import pallas as pl
from jax.experimental.pallas import tpu as pltpu
from jax.sharding import PartitionSpec as P

D = 4096
FF = 20480
BLOCK = 256
HALF = 128
ITERS = 6
DAMPING = 0.001
ROWS = 8
COLS = 16
RIGHT = 5
SHARE = 2 * BLOCK // ROWS
SLOT = BLOCK + 8 + SHARE
PACK = BLOCK + 8

f32 = jnp.float32
bf16 = jnp.bfloat16

def swap(value, d):
    return lax.ppermute(value, "col", [(i, i ^ d) for i in range(COLS)])


def exchanged(slots):
    return lax.all_to_all(slots, "row", split_axis=0, concat_axis=0, tiled=True)


def parts(value):
    high = value.astype(bf16)
    return high, (value - high.astype(f32)).astype(bf16)


def dot(left, right, dims=((1,), (0,))):
    return lax.dot_general(left, right, (dims, ((), ())), preferred_element_type=f32)


def product(left, right):
    (lh, ll), (rh, rl) = left, right
    return dot(lh, rh) + (dot(lh, rl) + dot(ll, rh))


def halves_product(left, right):
    return jnp.concatenate(
        [product([part[k : k + HALF] for part in left], right) for k in (0, HALF)], axis=0
    )


def iotas(n):
    return (
        lax.broadcasted_iota(jnp.int32, (n, n), 0),
        lax.broadcasted_iota(jnp.int32, (n, n), 1),
    )


def packed_parts(block):
    i, j = iotas(HALF)
    first, last = block[:HALF, :HALF], block[HALF:, HALF:]
    quarters = jnp.concatenate([block[:HALF, HALF:], jnp.where(i >= j, first, last)], axis=0)
    return quarters, jnp.sum(jnp.where(i == j, last, 0.0), axis=0, keepdims=True)


def packed_gram(even, odd):
    i, j = iotas(HALF)
    first, last = odd[:HALF, :HALF], odd[HALF:, HALF:]
    upper = even[:HALF, HALF:] + odd[:HALF, HALF:] + odd[HALF:, :HALF].T
    mixed = jnp.where(i >= j, even[:HALF, :HALF] + first, even[HALF:, HALF:] + last)
    mixed = mixed + jnp.where(i <= j, first, last).T
    diagonal = jnp.sum(jnp.where(i == j, even[HALF:, HALF:] + 2.0 * last, 0.0), axis=0, keepdims=True)
    return jnp.concatenate([upper, mixed], axis=0), diagonal


def store_packed(ref, start, block):
    quarters, diagonal = packed_parts(block)
    ref[pl.ds(start, BLOCK), :] = quarters
    ref[pl.ds(start + BLOCK, 8), :] = jnp.broadcast_to(diagonal, (8, HALF))


def unpacked(packed, diagonal=None):
    i, j = iotas(HALF)
    upper, mixed = packed[:HALF], packed[HALF:BLOCK]
    if diagonal is None:
        diagonal = packed[BLOCK : BLOCK + 1]
    turned = mixed.T
    first = jnp.where(i >= j, mixed, turned)
    last = jnp.where(i < j, mixed, jnp.where(i == j, jnp.broadcast_to(diagonal, (HALF, HALF)), turned))
    return jnp.concatenate(
        [
            jnp.concatenate([first, upper], axis=1),
            jnp.concatenate([upper.T, last], axis=1),
        ],
        axis=0,
    )


def root_steps(statistics, found):
    i, j = iotas(BLOCK)
    identity = jnp.where(i == j, 1.0, 0.0).astype(f32)
    currents, scaleds, squares = [], [], []
    for statistic in statistics:
        damped = statistic + DAMPING * identity
        split = parts(damped)
        square = halves_product(split, split)
        norm = jnp.sqrt(jnp.sum(damped * damped, axis=(0, 1), keepdims=True))
        inverse = 1.0 / norm
        scaled = damped * inverse
        currents.append(lax.rsqrt(jnp.sqrt(norm)))
        scaleds.append(scaled)
        squares.append(
            parts((25.0 / 16.0) * identity - (10.0 / 16.0) * scaled + (square * inverse) * (inverse * (1.0 / 16.0)))
        )
    yield
    for iteration in range(ITERS):
        factors = [(5.0 * identity - scaled) * 0.25 for scaled in scaleds]
        split = [parts(factor) for factor in factors]
        if iteration == ITERS - 1:
            found.extend(halves_product(parts(current), fs) for current, fs in zip(currents, split))
            return
        if iteration == 0:
            currents = [current * factor for current, factor in zip(currents, factors)]
        else:
            squares = [parts(halves_product(fs, fs)) for fs in split]
            yield
            currents = [halves_product(parts(current), fs) for current, fs in zip(currents, split)]
        fourths = [parts(halves_product(sq, sq)) for sq in squares]
        yield
        scaleds = [halves_product(fo, parts(scaled)) for fo, scaled in zip(fourths, scaleds)]
        yield


def roots(statistics):
    found = []
    for _ in root_steps(statistics, found):
        pass
    return found


def fetched(sources, buffer, sems):
    tiles = []
    for b in range(RIGHT):
        columns = pl.ds(b * BLOCK, BLOCK)
        tiles.append(
            [
                pltpu.make_async_copy(source.at[:, columns], buffer.at[s, b], sems.at[s, b])
                for s, source in enumerate(sources)
            ]
        )
    for copies in tiles:
        for copy in copies:
            copy.start()
    return tiles


def right_stats_kernel(first, second, out, buffer, sems):
    tiles = fetched((first, second), buffer, sems)
    half = ROWS // 2
    for group in ((0,), (1, 2), (3, 4)):
        for b in group:
            for copy in tiles[b]:
                copy.wait()
        packed = []
        for b in group:
            for s in range(2):
                high, low = parts(buffer[s, b])
                gram = dot(high, jnp.concatenate([high, low], axis=1), ((0,), (0,))) * (1.0 / D)
                packed.append(packed_gram(gram[:, :BLOCK], gram[:, BLOCK:]))
        for k, b in enumerate(group):
            one, two = packed[2 * k : 2 * k + 2]
            for s, (quarters, diagonal) in enumerate((one, (one[0] + two[0], one[1] + two[1]))):
                if b < RIGHT - 1:
                    out[2 * b + s, :BLOCK, :] = quarters
                    out[2 * b + s, BLOCK : BLOCK + 1, :] = diagonal
                else:
                    out[s * half : (s + 1) * half, BLOCK + 8 :, :] = quarters.reshape(half, SHARE, HALF)
                    for slot in range(ROWS):
                        out[slot, BLOCK + 1 + s : BLOCK + 2 + s, :] = diagonal
    for slot in range(ROWS):
        out[slot, BLOCK + 3 : BLOCK + 8, :] = jnp.zeros((5, HALF), f32)


def left_stats_kernel(info, first, second, keep, send, buffer, sums, sems):
    core = info[0]
    tiles = fetched((first, second), buffer, sems)
    for b in range(RIGHT):
        for copy in tiles[b]:
            copy.wait()
        for s in range(2):
            for block in range(2):
                high, low = parts(buffer[s, b, block * BLOCK : (block + 1) * BLOCK, :])
                gram = dot(high, jnp.concatenate([high, low], axis=0), ((1,), (1,)))
                if b == 0:
                    sums[block, s] = gram
                else:
                    sums[block, s] += gram
    for out, block in ((keep, core), (send, 1 - core)):
        total = None
        for s in range(2):
            gram = sums[block, s] * (1.0 / FF)
            gram = packed_gram(gram[:, :BLOCK], gram[:, BLOCK:])
            total = gram if s == 0 else (total[0] + gram[0], total[1] + gram[1])
            out[s * PACK : s * PACK + BLOCK, :] = total[0]
            out[s * PACK + BLOCK : (s + 1) * PACK, :] = jnp.broadcast_to(total[1], (8, HALF))


def right_roots_kernel(arrived, right_out, diagonals, buffer, sems):
    copies = [pltpu.make_async_copy(arrived.at[slot], buffer.at[slot], sems.at[slot]) for slot in range(ROWS)]
    for copy in copies:
        copy.start()
    copies[0].wait()
    total = buffer[0]
    for slot in range(1, ROWS):
        copies[slot].wait()
        total = total + buffer[slot]
    for slot in range(ROWS):
        right_out[slot, PACK:, :] = total[PACK:]
    diagonals[...] = total[BLOCK:PACK]
    (root,) = roots([unpacked(total[:PACK])])
    quarters, diagonal = packed_parts(root)
    for slot in range(ROWS):
        right_out[slot, :BLOCK, :] = quarters
        right_out[slot, BLOCK:PACK, :] = jnp.broadcast_to(diagonal, (8, HALF))


def left_root_kernel(own, other, out):
    (root,) = roots([unpacked(own[...] + other[...])])
    store_packed(out, 0, root)


def halfway_kernel(info, first, second, mine, other, out, buffer, results, sems, out_sems):
    core = info[0]
    tiles = fetched((first, second), buffer, sems)
    split = [[parts(unpacked(ref[s * PACK : (s + 1) * PACK, :])) for s in range(2)] for ref in (mine, other)]
    copies = []
    for b in range(RIGHT):
        for copy in tiles[b]:
            copy.wait()
        for s in range(2):
            for place, block in enumerate((core, 1 - core)):
                rows = pl.ds(pl.multiple_of(block * BLOCK, BLOCK), BLOCK)
                result = product(split[place][s], parts(buffer[s, b, rows, :]))
                results[b, 2 * s, rows, :], results[b, 2 * s + 1, rows, :] = parts(result)
        copy = pltpu.make_async_copy(results.at[b], out.at[b], out_sems.at[b])
        copy.start()
        copies.append(copy)
    for copy in copies:
        copy.wait()


def applied(held, b, one, two, buffer):
    (h1, l1), (h2, l2) = one, two
    weights = jnp.concatenate([h1, h1, l1, h2, h2, l2], axis=0)
    for start in (0, BLOCK):
        rows = slice(start, start + BLOCK)
        high_one, low_one, high_two, low_two = [held[b, q, rows, :] for q in range(4)]
        lhs = jnp.concatenate([low_one, high_one, high_one, low_two, high_two, high_two], axis=1)
        buffer[b, rows, :] = dot(lhs, weights)
        yield


def finish_kernel(
    halfway, gathered, diagonals, out, held, roots_in, shares, buffer, sems, root_sems, share_sem, out_sems
):
    share_copy = pltpu.make_async_copy(gathered.at[:, pl.ds(PACK, SHARE), :], shares, share_sem)
    share_copy.start()
    fetches = []
    for b in range(RIGHT):
        fetches.append([])
        if b < RIGHT - 1:
            pair = pl.ds(2 * b, 2)
            fetches[b].append(
                pltpu.make_async_copy(
                    gathered.at[pair, pl.ds(0, PACK), :], roots_in.at[pair], root_sems.at[b]
                )
            )
        fetches[b].append(pltpu.make_async_copy(halfway.at[b], held.at[b], sems.at[b]))
        for copy in fetches[b]:
            copy.start()
    half = ROWS // 2
    share_copy.wait()
    statistics = [
        unpacked(shares[s * half : (s + 1) * half].reshape(BLOCK, HALF), diagonals[1 + s : 2 + s, :])
        for s in range(2)
    ]
    found = []
    chain = root_steps(statistics, found)
    copies = []

    def stored(b):
        copy = pltpu.make_async_copy(buffer.at[b], out.at[:, pl.ds(b * BLOCK, BLOCK)], out_sems.at[b])
        copy.start()
        copies.append(copy)

    for _ in range(4):
        next(chain)
    for b in range(RIGHT - 1):
        for copy in fetches[b]:
            copy.wait()
    for b in range(RIGHT - 1):
        one, two = parts(unpacked(roots_in[2 * b])), parts(unpacked(roots_in[2 * b + 1]))
        for _ in applied(held, b, one, two, buffer):
            next(chain, None)
        stored(b)
        next(chain, None)
    for _ in chain:
        pass
    last = RIGHT - 1
    fetches[last][0].wait()
    for _ in applied(held, last, parts(found[0]), parts(found[1]), buffer):
        pass
    stored(last)
    for copy in copies:
        copy.wait()


VMEM = pl.BlockSpec(memory_space=pltpu.VMEM)
SMEM = pl.BlockSpec(memory_space=pltpu.SMEM)
HBM = pl.BlockSpec(memory_space=pltpu.HBM)
ANY = pl.BlockSpec(memory_space=pl.ANY)


def in_hbm(*values):
    return [pltpu.with_memory_space_constraint(value, pltpu.HBM) for value in values]


def params():
    return pltpu.CompilerParams(vmem_limit_bytes=32 * 1024 * 1024)


def cost(flops, moved):
    return pl.CostEstimate(flops=int(flops), bytes_accessed=int(moved), transcendentals=0)


def body(grad_first, grad_second):
    rows, cols = grad_first.shape
    col = lax.axis_index("col")
    core = lax.rem(col, 2)
    low_y = lax.rem(col // 4, 2)
    info = core.reshape(1).astype(jnp.int32)
    pair = jax.ShapeDtypeStruct((2 * PACK, HALF), f32)
    single = jax.ShapeDtypeStruct((PACK, HALF), f32)
    grads = 2 * rows * cols * 4
    passes = 3 * 2 * BLOCK * rows * cols * 2
    newton = 20 * 6 * BLOCK**3
    tiles = [pltpu.VMEM((2, RIGHT, rows, BLOCK), f32)]
    tile_sems = [pltpu.SemaphoreType.DMA((2, RIGHT))]

    right_parts = pl.pallas_call(
        right_stats_kernel,
        in_specs=[HBM, HBM],
        out_specs=VMEM,
        out_shape=jax.ShapeDtypeStruct((ROWS, SLOT, HALF), f32),
        scratch_shapes=tiles + tile_sems,
        compiler_params=params(),
        cost_estimate=cost(passes, grads),
        name="right_stats",
    )(*in_hbm(grad_first, grad_second))
    arrived = exchanged(right_parts)

    info, right_parts = lax.optimization_barrier((info, right_parts))
    keep, send = pl.pallas_call(
        left_stats_kernel,
        in_specs=[SMEM, HBM, HBM],
        out_specs=[VMEM, VMEM],
        out_shape=[pair, pair],
        scratch_shapes=tiles + [pltpu.VMEM((2, 2, BLOCK, 2 * BLOCK), f32)] + tile_sems,
        compiler_params=params(),
        cost_estimate=cost(passes, grads),
        name="left_stats",
    )(info, *in_hbm(grad_first, grad_second))
    both = (keep + swap(send, 1)).reshape(2, PACK, HALF)
    own = lax.dynamic_index_in_dim(both, low_y, 0, keepdims=False)
    rest = lax.dynamic_index_in_dim(both, 1 - low_y, 0, keepdims=False)
    own = (own + swap(rest, 4)) + (swap(own, 8) + swap(rest, 12))
    own, arrived = lax.optimization_barrier((own, arrived))
    left_in = [own, swap(own, 2)]

    slots = jax.ShapeDtypeStruct((ROWS, SLOT, HALF), f32)
    right_root, diagonals = pl.pallas_call(
        right_roots_kernel,
        in_specs=[ANY],
        out_specs=[VMEM, VMEM],
        out_shape=[slots, jax.ShapeDtypeStruct((8, HALF), f32)],
        scratch_shapes=[pltpu.VMEM((ROWS, SLOT, HALF), f32), pltpu.SemaphoreType.DMA((ROWS,))],
        compiler_params=params(),
        cost_estimate=cost(newton, 2 * ROWS * SLOT * HALF * 4),
        name="right_roots",
    )(arrived)
    left_in, right_root = lax.optimization_barrier((left_in, right_root))
    gathered = exchanged(right_root)
    left_in, right_root = lax.optimization_barrier((left_in, right_root))
    left_root = pl.pallas_call(
        left_root_kernel,
        in_specs=[VMEM, VMEM],
        out_specs=VMEM,
        out_shape=single,
        compiler_params=params(),
        cost_estimate=cost(newton, 3 * PACK * HALF * 4),
        name="left_root",
    )(*left_in)
    left_other = swap(left_root, 4)
    mine = jnp.where(
        low_y == 0,
        jnp.concatenate([left_root, left_other]),
        jnp.concatenate([left_other, left_root]),
    )
    other = swap(mine, 1)

    held = (RIGHT, 4, rows, BLOCK)
    tile_sem = pltpu.SemaphoreType.DMA((RIGHT,))
    halfway = pl.pallas_call(
        halfway_kernel,
        in_specs=[SMEM, HBM, HBM, VMEM, VMEM],
        out_specs=HBM,
        out_shape=pltpu.HBM(held, bf16),
        scratch_shapes=tiles + [pltpu.VMEM(held, bf16)] + tile_sems + [tile_sem],
        compiler_params=params(),
        cost_estimate=cost(passes, 2 * grads),
        name="halfway",
    )(info, *in_hbm(grad_first, grad_second), mine, other)

    return pl.pallas_call(
        finish_kernel,
        in_specs=[HBM, ANY, VMEM],
        out_specs=HBM,
        scratch_shapes=[
            pltpu.VMEM(held, bf16),
            pltpu.VMEM((ROWS, PACK, HALF), f32),
            pltpu.VMEM((ROWS, SHARE, HALF), f32),
            pltpu.VMEM((RIGHT, rows, BLOCK), f32),
            tile_sem,
            tile_sem,
            pltpu.SemaphoreType.DMA(()),
            tile_sem,
        ],
        out_shape=jax.ShapeDtypeStruct((rows, cols), f32),
        compiler_params=params(),
        cost_estimate=cost(passes + 2 * newton, 2 * grads),
        name="finish",
    )(*in_hbm(halfway), gathered, diagonals)


def solution(mesh):
    in_specs = (P("row", "col"), P("row", "col"))
    out_specs = P("row", "col")
    return jax.shard_map(body, mesh=mesh, in_specs=in_specs, out_specs=out_specs, check_vma=False)
```

```python
import jax
import jax.numpy as jnp
from jax import lax
from jax.experimental import pallas as pl
from jax.experimental.pallas import tpu as pltpu
from jax.sharding import PartitionSpec as P

D = 4096
FF = 20480
BLOCK = 256
HALF = 128
ITERS = 6
DAMPING = 0.001
ROWS = 8
COLS = 16
RIGHT = 5
SHARE = 2 * BLOCK // ROWS
SLOT = BLOCK + 8 + SHARE
PACK = BLOCK + 8

f32 = jnp.float32
bf16 = jnp.bfloat16

def swap(value, d):
    return lax.ppermute(value, "col", [(i, i ^ d) for i in range(COLS)])


def exchanged(slots):
    return lax.all_to_all(slots, "row", split_axis=0, concat_axis=0, tiled=True)


def parts(value):
    high = value.astype(bf16)
    return high, (value - high.astype(f32)).astype(bf16)


def dot(left, right, dims=((1,), (0,))):
    return lax.dot_general(left, right, (dims, ((), ())), preferred_element_type=f32)


def product(left, right):
    (lh, ll), (rh, rl) = left, right
    return dot(lh, rh) + (dot(lh, rl) + dot(ll, rh))


def halves_product(left, right):
    return jnp.concatenate(
        [product([part[k : k + HALF] for part in left], right) for k in (0, HALF)], axis=0
    )


def iotas(n):
    return (
        lax.broadcasted_iota(jnp.int32, (n, n), 0),
        lax.broadcasted_iota(jnp.int32, (n, n), 1),
    )


def packed_parts(block):
    i, j = iotas(HALF)
    first, last = block[:HALF, :HALF], block[HALF:, HALF:]
    quarters = jnp.concatenate([block[:HALF, HALF:], jnp.where(i >= j, first, last)], axis=0)
    return quarters, jnp.sum(jnp.where(i == j, last, 0.0), axis=0, keepdims=True)


def packed_gram(even, odd):
    i, j = iotas(HALF)
    first, last = odd[:HALF, :HALF], odd[HALF:, HALF:]
    upper = even[:HALF, HALF:] + odd[:HALF, HALF:] + odd[HALF:, :HALF].T
    mixed = jnp.where(i >= j, even[:HALF, :HALF] + first, even[HALF:, HALF:] + last)
    mixed = mixed + jnp.where(i <= j, first, last).T
    diagonal = jnp.sum(jnp.where(i == j, even[HALF:, HALF:] + 2.0 * last, 0.0), axis=0, keepdims=True)
    return jnp.concatenate([upper, mixed], axis=0), diagonal


def store_packed(ref, start, block):
    quarters, diagonal = packed_parts(block)
    ref[pl.ds(start, BLOCK), :] = quarters
    ref[pl.ds(start + BLOCK, 8), :] = jnp.broadcast_to(diagonal, (8, HALF))


def unpacked(packed, diagonal=None):
    i, j = iotas(HALF)
    upper, mixed = packed[:HALF], packed[HALF:BLOCK]
    if diagonal is None:
        diagonal = packed[BLOCK : BLOCK + 1]
    turned = mixed.T
    first = jnp.where(i >= j, mixed, turned)
    last = jnp.where(i < j, mixed, jnp.where(i == j, jnp.broadcast_to(diagonal, (HALF, HALF)), turned))
    return jnp.concatenate(
        [
            jnp.concatenate([first, upper], axis=1),
            jnp.concatenate([upper.T, last], axis=1),
        ],
        axis=0,
    )


def root_steps(statistics, found):
    i, j = iotas(BLOCK)
    identity = jnp.where(i == j, 1.0, 0.0).astype(f32)
    currents, scaleds, squares = [], [], []
    for statistic in statistics:
        damped = statistic + DAMPING * identity
        split = parts(damped)
        square = halves_product(split, split)
        norm = jnp.sqrt(jnp.sum(damped * damped, axis=(0, 1), keepdims=True))
        inverse = 1.0 / norm
        scaled = damped * inverse
        currents.append(lax.rsqrt(jnp.sqrt(norm)))
        scaleds.append(scaled)
        squares.append(
            parts((25.0 / 16.0) * identity - (10.0 / 16.0) * scaled + (square * inverse) * (inverse * (1.0 / 16.0)))
        )
    yield
    for iteration in range(ITERS):
        factors = [(5.0 * identity - scaled) * 0.25 for scaled in scaleds]
        split = [parts(factor) for factor in factors]
        if iteration == ITERS - 1:
            found.extend(halves_product(parts(current), fs) for current, fs in zip(currents, split))
            return
        if iteration == 0:
            currents = [current * factor for current, factor in zip(currents, factors)]
        else:
            squares = [parts(halves_product(fs, fs)) for fs in split]
            yield
            currents = [halves_product(parts(current), fs) for current, fs in zip(currents, split)]
        fourths = [parts(halves_product(sq, sq)) for sq in squares]
        yield
        scaleds = [halves_product(fo, parts(scaled)) for fo, scaled in zip(fourths, scaleds)]
        yield


def roots(statistics):
    found = []
    for _ in root_steps(statistics, found):
        pass
    return found


def fetched(sources, buffer, sems):
    tiles = []
    for b in range(RIGHT):
        columns = pl.ds(b * BLOCK, BLOCK)
        tiles.append(
            [
                pltpu.make_async_copy(source.at[:, columns], buffer.at[s, b], sems.at[s, b])
                for s, source in enumerate(sources)
            ]
        )
    for copies in tiles:
        for copy in copies:
            copy.start()
    return tiles


def right_stats_kernel(first, second, out, buffer, sems):
    tiles = fetched((first, second), buffer, sems)
    half = ROWS // 2
    for group in ((0,), (1, 2), (3, 4)):
        for b in group:
            for copy in tiles[b]:
                copy.wait()
        packed = []
        for b in group:
            for s in range(2):
                high, low = parts(buffer[s, b])
                gram = dot(high, jnp.concatenate([high, low], axis=1), ((0,), (0,))) * (1.0 / D)
                packed.append(packed_gram(gram[:, :BLOCK], gram[:, BLOCK:]))
        for k, b in enumerate(group):
            one, two = packed[2 * k : 2 * k + 2]
            for s, (quarters, diagonal) in enumerate((one, (one[0] + two[0], one[1] + two[1]))):
                if b < RIGHT - 1:
                    out[2 * b + s, :BLOCK, :] = quarters
                    out[2 * b + s, BLOCK : BLOCK + 1, :] = diagonal
                else:
                    out[s * half : (s + 1) * half, BLOCK + 8 :, :] = quarters.reshape(half, SHARE, HALF)
                    for slot in range(ROWS):
                        out[slot, BLOCK + 1 + s : BLOCK + 2 + s, :] = diagonal
    for slot in range(ROWS):
        out[slot, BLOCK + 3 : BLOCK + 8, :] = jnp.zeros((5, HALF), f32)


def left_stats_kernel(info, first, second, keep, send, buffer, sums, sems):
    core = info[0]
    tiles = fetched((first, second), buffer, sems)
    for b in range(RIGHT):
        for copy in tiles[b]:
            copy.wait()
        for s in range(2):
            for block in range(2):
                high, low = parts(buffer[s, b, block * BLOCK : (block + 1) * BLOCK, :])
                gram = dot(high, jnp.concatenate([high, low], axis=0), ((1,), (1,)))
                if b == 0:
                    sums[block, s] = gram
                else:
                    sums[block, s] += gram
    for out, block in ((keep, core), (send, 1 - core)):
        total = None
        for s in range(2):
            gram = sums[block, s] * (1.0 / FF)
            gram = packed_gram(gram[:, :BLOCK], gram[:, BLOCK:])
            total = gram if s == 0 else (total[0] + gram[0], total[1] + gram[1])
            out[s * PACK : s * PACK + BLOCK, :] = total[0]
            out[s * PACK + BLOCK : (s + 1) * PACK, :] = jnp.broadcast_to(total[1], (8, HALF))


def right_roots_kernel(arrived, right_out, diagonals):
    total = arrived[0]
    for slot in range(1, ROWS):
        total = total + arrived[slot]
    for slot in range(ROWS):
        right_out[slot, PACK:, :] = total[PACK:]
    diagonals[...] = total[BLOCK:PACK]
    (root,) = roots([unpacked(total[:PACK])])
    quarters, diagonal = packed_parts(root)
    for slot in range(ROWS):
        right_out[slot, :BLOCK, :] = quarters
        right_out[slot, BLOCK:PACK, :] = jnp.broadcast_to(diagonal, (8, HALF))


def left_root_kernel(own, other, out):
    (root,) = roots([unpacked(own[...] + other[...])])
    store_packed(out, 0, root)


def halfway_kernel(info, first, second, mine, other, out, buffer, results, sems, out_sems):
    core = info[0]
    tiles = fetched((first, second), buffer, sems)
    split = [[parts(unpacked(ref[s * PACK : (s + 1) * PACK, :])) for s in range(2)] for ref in (mine, other)]
    copies = []
    for b in range(RIGHT):
        for copy in tiles[b]:
            copy.wait()
        for s in range(2):
            for place, block in enumerate((core, 1 - core)):
                rows = pl.ds(pl.multiple_of(block * BLOCK, BLOCK), BLOCK)
                result = product(split[place][s], parts(buffer[s, b, rows, :]))
                results[b, 2 * s, rows, :], results[b, 2 * s + 1, rows, :] = parts(result)
        copy = pltpu.make_async_copy(results.at[b], out.at[b], out_sems.at[b])
        copy.start()
        copies.append(copy)
    for copy in copies:
        copy.wait()


def applied(held, b, one, two, buffer):
    (h1, l1), (h2, l2) = one, two
    weights = jnp.concatenate([h1, h1, l1, h2, h2, l2], axis=0)
    for start in (0, BLOCK):
        rows = slice(start, start + BLOCK)
        high_one, low_one, high_two, low_two = [held[b, q, rows, :] for q in range(4)]
        lhs = jnp.concatenate([low_one, high_one, high_one, low_two, high_two, high_two], axis=1)
        buffer[b, rows, :] = dot(lhs, weights)
        yield


def finish_kernel(
    halfway, gathered, diagonals, out, held, buffer, sems, out_sems
):
    fetches = [pltpu.make_async_copy(halfway.at[b], held.at[b], sems.at[b]) for b in range(RIGHT)]
    for copy in fetches:
        copy.start()
    half = ROWS // 2
    statistics = [
        unpacked(gathered[s * half : (s + 1) * half, PACK:, :].reshape(BLOCK, HALF), diagonals[1 + s : 2 + s, :])
        for s in range(2)
    ]
    found = []
    chain = root_steps(statistics, found)
    copies = []

    def stored(b):
        copy = pltpu.make_async_copy(buffer.at[b], out.at[:, pl.ds(b * BLOCK, BLOCK)], out_sems.at[b])
        copy.start()
        copies.append(copy)

    for _ in range(4):
        next(chain)
    for copy in fetches:
        copy.wait()
    for b in range(RIGHT - 1):
        one, two = [parts(unpacked(gathered[2 * b + s, :PACK, :])) for s in range(2)]
        for _ in applied(held, b, one, two, buffer):
            next(chain, None)
        stored(b)
        next(chain, None)
    for _ in chain:
        pass
    last = RIGHT - 1
    for _ in applied(held, last, parts(found[0]), parts(found[1]), buffer):
        pass
    stored(last)
    for copy in copies:
        copy.wait()


VMEM = pl.BlockSpec(memory_space=pltpu.VMEM)
SMEM = pl.BlockSpec(memory_space=pltpu.SMEM)
HBM = pl.BlockSpec(memory_space=pltpu.HBM)


def in_hbm(*values):
    return [pltpu.with_memory_space_constraint(value, pltpu.HBM) for value in values]


def params():
    return pltpu.CompilerParams(vmem_limit_bytes=32 * 1024 * 1024)


def cost(flops, moved):
    return pl.CostEstimate(flops=int(flops), bytes_accessed=int(moved), transcendentals=0)


def body(grad_first, grad_second):
    rows, cols = grad_first.shape
    col = lax.axis_index("col")
    core = lax.rem(col, 2)
    low_y = lax.rem(col // 4, 2)
    info = core.reshape(1).astype(jnp.int32)
    pair = jax.ShapeDtypeStruct((2 * PACK, HALF), f32)
    single = jax.ShapeDtypeStruct((PACK, HALF), f32)
    grads = 2 * rows * cols * 4
    passes = 3 * 2 * BLOCK * rows * cols * 2
    newton = 20 * 6 * BLOCK**3
    tiles = [pltpu.VMEM((2, RIGHT, rows, BLOCK), f32)]
    tile_sems = [pltpu.SemaphoreType.DMA((2, RIGHT))]

    right_parts = pl.pallas_call(
        right_stats_kernel,
        in_specs=[HBM, HBM],
        out_specs=VMEM,
        out_shape=jax.ShapeDtypeStruct((ROWS, SLOT, HALF), f32),
        scratch_shapes=tiles + tile_sems,
        compiler_params=params(),
        cost_estimate=cost(passes, grads),
        name="right_stats",
    )(*in_hbm(grad_first, grad_second))
    arrived = exchanged(right_parts)

    info, right_parts = lax.optimization_barrier((info, right_parts))
    keep, send = pl.pallas_call(
        left_stats_kernel,
        in_specs=[SMEM, HBM, HBM],
        out_specs=[VMEM, VMEM],
        out_shape=[pair, pair],
        scratch_shapes=tiles + [pltpu.VMEM((2, 2, BLOCK, 2 * BLOCK), f32)] + tile_sems,
        compiler_params=params(),
        cost_estimate=cost(passes, grads),
        name="left_stats",
    )(info, *in_hbm(grad_first, grad_second))
    both = (keep + swap(send, 1)).reshape(2, PACK, HALF)
    own = lax.dynamic_index_in_dim(both, low_y, 0, keepdims=False)
    rest = lax.dynamic_index_in_dim(both, 1 - low_y, 0, keepdims=False)
    own = (own + swap(rest, 4)) + (swap(own, 8) + swap(rest, 12))
    left_in = [own, swap(own, 2)]
    own, arrived = lax.optimization_barrier((own, arrived))

    right_root, diagonals = pl.pallas_call(
        right_roots_kernel,
        in_specs=[VMEM],
        out_specs=[VMEM, VMEM],
        out_shape=[jax.ShapeDtypeStruct((ROWS, SLOT, HALF), f32), jax.ShapeDtypeStruct((8, HALF), f32)],
        compiler_params=params(),
        cost_estimate=cost(newton, 2 * ROWS * SLOT * HALF * 4),
        name="right_roots",
    )(arrived)
    left_in, right_root = lax.optimization_barrier((left_in, right_root))
    gathered = exchanged(right_root)
    left_in, right_root = lax.optimization_barrier((left_in, right_root))
    left_root = pl.pallas_call(
        left_root_kernel,
        in_specs=[VMEM, VMEM],
        out_specs=VMEM,
        out_shape=single,
        compiler_params=params(),
        cost_estimate=cost(newton, 3 * PACK * HALF * 4),
        name="left_root",
    )(*left_in)
    left_other = swap(left_root, 4)
    mine = jnp.where(
        low_y == 0,
        jnp.concatenate([left_root, left_other]),
        jnp.concatenate([left_other, left_root]),
    )
    other = swap(mine, 1)

    held = (RIGHT, 4, rows, BLOCK)
    tile_sem = pltpu.SemaphoreType.DMA((RIGHT,))
    halfway = pl.pallas_call(
        halfway_kernel,
        in_specs=[SMEM, HBM, HBM, VMEM, VMEM],
        out_specs=HBM,
        out_shape=pltpu.HBM(held, bf16),
        scratch_shapes=tiles + [pltpu.VMEM(held, bf16)] + tile_sems + [tile_sem],
        compiler_params=params(),
        cost_estimate=cost(passes, 2 * grads),
        name="halfway",
    )(info, *in_hbm(grad_first, grad_second), mine, other)

    return pl.pallas_call(
        finish_kernel,
        in_specs=[HBM, VMEM, VMEM],
        out_specs=HBM,
        scratch_shapes=[
            pltpu.VMEM(held, bf16),
            pltpu.VMEM((RIGHT, rows, BLOCK), f32),
            tile_sem,
            tile_sem,
        ],
        out_shape=jax.ShapeDtypeStruct((rows, cols), f32),
        compiler_params=params(),
        cost_estimate=cost(passes + 2 * newton, 2 * grads),
        name="finish",
    )(*in_hbm(halfway), gathered, diagonals)


def solution(mesh):
    in_specs = (P("row", "col"), P("row", "col"))
    out_specs = P("row", "col")
    return jax.shard_map(body, mesh=mesh, in_specs=in_specs, out_specs=out_specs, check_vma=False)
```

```python
import jax
import jax.numpy as jnp
from jax import lax
from jax.experimental import pallas as pl
from jax.experimental.pallas import tpu as pltpu
from jax.sharding import PartitionSpec as P

D = 4096
FF = 20480
BLOCK = 256
HALF = 128
ITERS = 6
DAMPING = 0.001
ROWS = 8
COLS = 16
RIGHT = 5
SHARE = 2 * BLOCK // ROWS
SLOT = BLOCK + 8 + SHARE
PACK = BLOCK + 8

f32 = jnp.float32
bf16 = jnp.bfloat16

def swap(value, d):
    return lax.ppermute(value, "col", [(i, i ^ d) for i in range(COLS)])


def exchanged(slots):
    return lax.all_to_all(slots, "row", split_axis=0, concat_axis=0, tiled=True)


def parts(value):
    high = value.astype(bf16)
    return high, (value - high.astype(f32)).astype(bf16)


def dot(left, right, dims=((1,), (0,))):
    return lax.dot_general(left, right, (dims, ((), ())), preferred_element_type=f32)


def product(left, right):
    (lh, ll), (rh, rl) = left, right
    return dot(lh, rh) + (dot(lh, rl) + dot(ll, rh))


def halves_product(left, right):
    return jnp.concatenate(
        [product([part[k : k + HALF] for part in left], right) for k in (0, HALF)], axis=0
    )


def iotas(n):
    return (
        lax.broadcasted_iota(jnp.int32, (n, n), 0),
        lax.broadcasted_iota(jnp.int32, (n, n), 1),
    )


def packed_parts(block):
    i, j = iotas(HALF)
    first, last = block[:HALF, :HALF], block[HALF:, HALF:]
    quarters = jnp.concatenate([block[:HALF, HALF:], jnp.where(i >= j, first, last)], axis=0)
    return quarters, jnp.sum(jnp.where(i == j, last, 0.0), axis=0, keepdims=True)


def packed_gram(even, odd):
    i, j = iotas(HALF)
    first, last = odd[:HALF, :HALF], odd[HALF:, HALF:]
    upper = even[:HALF, HALF:] + odd[:HALF, HALF:] + odd[HALF:, :HALF].T
    mixed = jnp.where(i >= j, even[:HALF, :HALF] + first, even[HALF:, HALF:] + last)
    mixed = mixed + jnp.where(i <= j, first, last).T
    diagonal = jnp.sum(jnp.where(i == j, even[HALF:, HALF:] + 2.0 * last, 0.0), axis=0, keepdims=True)
    return jnp.concatenate([upper, mixed], axis=0), diagonal


def store_packed(ref, start, block):
    quarters, diagonal = packed_parts(block)
    ref[pl.ds(start, BLOCK), :] = quarters
    ref[pl.ds(start + BLOCK, 8), :] = jnp.broadcast_to(diagonal, (8, HALF))


def unpacked(packed, diagonal=None):
    i, j = iotas(HALF)
    upper, mixed = packed[:HALF], packed[HALF:BLOCK]
    if diagonal is None:
        diagonal = packed[BLOCK : BLOCK + 1]
    turned = mixed.T
    first = jnp.where(i >= j, mixed, turned)
    last = jnp.where(i < j, mixed, jnp.where(i == j, jnp.broadcast_to(diagonal, (HALF, HALF)), turned))
    return jnp.concatenate(
        [
            jnp.concatenate([first, upper], axis=1),
            jnp.concatenate([upper.T, last], axis=1),
        ],
        axis=0,
    )


def root_steps(statistics, found):
    i, j = iotas(BLOCK)
    identity = jnp.where(i == j, 1.0, 0.0).astype(f32)
    currents, scaleds, squares = [], [], []
    for statistic in statistics:
        damped = statistic + DAMPING * identity
        split = parts(damped)
        square = halves_product(split, split)
        norm = jnp.sqrt(jnp.sum(damped * damped, axis=(0, 1), keepdims=True))
        inverse = 1.0 / norm
        scaled = damped * inverse
        currents.append(lax.rsqrt(jnp.sqrt(norm)))
        scaleds.append(scaled)
        squares.append(
            parts((25.0 / 16.0) * identity - (10.0 / 16.0) * scaled + (square * inverse) * (inverse * (1.0 / 16.0)))
        )
    yield
    for iteration in range(ITERS):
        factors = [(5.0 * identity - scaled) * 0.25 for scaled in scaleds]
        split = [parts(factor) for factor in factors]
        if iteration == ITERS - 1:
            found.extend(halves_product(parts(current), fs) for current, fs in zip(currents, split))
            return
        if iteration == 0:
            currents = [current * factor for current, factor in zip(currents, factors)]
        else:
            squares = [parts(halves_product(fs, fs)) for fs in split]
            yield
            currents = [halves_product(parts(current), fs) for current, fs in zip(currents, split)]
        fourths = [parts(halves_product(sq, sq)) for sq in squares]
        yield
        scaleds = [halves_product(fo, parts(scaled)) for fo, scaled in zip(fourths, scaleds)]
        yield


def roots(statistics):
    found = []
    for _ in root_steps(statistics, found):
        pass
    return found


def fetched(sources, buffer, sems, order=range(RIGHT)):
    tiles = {}
    for b in order:
        columns = pl.ds(b * BLOCK, BLOCK)
        tiles[b] = [
            pltpu.make_async_copy(source.at[:, columns], buffer.at[s, b], sems.at[s, b])
            for s, source in enumerate(sources)
        ]
        for copy in tiles[b]:
            copy.start()
    return tiles


def right_stats_kernel(first, second, out, buffer, slots, sems, out_sems):
    groups = ((RIGHT - 1,), (0, 1), (2, 3))
    tiles = fetched((first, second), buffer, sems, sum(groups, ()))
    half = ROWS // 2
    copies = []
    for slot in range(ROWS):
        slots[slot, BLOCK + 3 : BLOCK + 8, :] = jnp.zeros((5, HALF), f32)
    for group in groups:
        for b in group:
            for copy in tiles[b]:
                copy.wait()
        packed = []
        for b in group:
            for s in range(2):
                high, low = parts(buffer[s, b])
                gram = dot(high, jnp.concatenate([high, low], axis=1), ((0,), (0,))) * (1.0 / D)
                packed.append(packed_gram(gram[:, :BLOCK], gram[:, BLOCK:]))
        for k, b in enumerate(group):
            one, two = packed[2 * k : 2 * k + 2]
            for s, (quarters, diagonal) in enumerate((one, (one[0] + two[0], one[1] + two[1]))):
                if b < RIGHT - 1:
                    slots[2 * b + s, :BLOCK, :] = quarters
                    slots[2 * b + s, BLOCK : BLOCK + 1, :] = diagonal
                else:
                    slots[s * half : (s + 1) * half, BLOCK + 8 :, :] = quarters.reshape(half, SHARE, HALF)
                    for slot in range(ROWS):
                        slots[slot, BLOCK + 1 + s : BLOCK + 2 + s, :] = diagonal
        for b in group:
            if b < RIGHT - 1:
                pair = pl.ds(2 * b, 2)
                copies.append(pltpu.make_async_copy(slots.at[pair], out.at[pair], out_sems.at[b]))
                copies[-1].start()
    for copy in copies:
        copy.wait()


def left_stats_kernel(info, first, second, keep, send, buffer, sums, sems):
    core = info[0]
    tiles = fetched((first, second), buffer, sems)
    for b in range(RIGHT):
        for copy in tiles[b]:
            copy.wait()
        for s in range(2):
            for block in range(2):
                high, low = parts(buffer[s, b, block * BLOCK : (block + 1) * BLOCK, :])
                gram = dot(high, jnp.concatenate([high, low], axis=0), ((1,), (1,)))
                if b == 0:
                    sums[block, s] = gram
                else:
                    sums[block, s] += gram
    for out, block in ((keep, core), (send, 1 - core)):
        total = None
        for s in range(2):
            gram = sums[block, s] * (1.0 / FF)
            gram = packed_gram(gram[:, :BLOCK], gram[:, BLOCK:])
            total = gram if s == 0 else (total[0] + gram[0], total[1] + gram[1])
            out[s * PACK : s * PACK + BLOCK, :] = total[0]
            out[s * PACK + BLOCK : (s + 1) * PACK, :] = jnp.broadcast_to(total[1], (8, HALF))


def right_roots_kernel(arrived, right_out, diagonals):
    total = arrived[0]
    for slot in range(1, ROWS):
        total = total + arrived[slot]
    for slot in range(ROWS):
        right_out[slot, PACK:, :] = total[PACK:]
    diagonals[...] = total[BLOCK:PACK]
    (root,) = roots([unpacked(total[:PACK])])
    quarters, diagonal = packed_parts(root)
    for slot in range(ROWS):
        right_out[slot, :BLOCK, :] = quarters
        right_out[slot, BLOCK:PACK, :] = jnp.broadcast_to(diagonal, (8, HALF))


def left_root_kernel(own, other, out):
    (root,) = roots([unpacked(own[...] + other[...])])
    store_packed(out, 0, root)


def halfway_kernel(info, first, second, mine, other, out, buffer, results, sems, out_sems):
    core = info[0]
    tiles = fetched((first, second), buffer, sems)
    split = [[parts(unpacked(ref[s * PACK : (s + 1) * PACK, :])) for s in range(2)] for ref in (mine, other)]
    copies = []
    for b in range(RIGHT):
        for copy in tiles[b]:
            copy.wait()
        for s in range(2):
            for place, block in enumerate((core, 1 - core)):
                rows = pl.ds(pl.multiple_of(block * BLOCK, BLOCK), BLOCK)
                result = product(split[place][s], parts(buffer[s, b, rows, :]))
                results[b, 2 * s, rows, :], results[b, 2 * s + 1, rows, :] = parts(result)
        copy = pltpu.make_async_copy(results.at[b], out.at[b], out_sems.at[b])
        copy.start()
        copies.append(copy)
    for copy in copies:
        copy.wait()


def applied(held, b, one, two, buffer):
    (h1, l1), (h2, l2) = one, two
    weights = jnp.concatenate([h1, h1, l1, h2, h2, l2], axis=0)
    for start in (0, BLOCK):
        rows = slice(start, start + BLOCK)
        high_one, low_one, high_two, low_two = [held[b, q, rows, :] for q in range(4)]
        lhs = jnp.concatenate([low_one, high_one, high_one, low_two, high_two, high_two], axis=1)
        buffer[b, rows, :] = dot(lhs, weights)
        yield


def finish_kernel(
    halfway, gathered, diagonals, out, held, buffer, sems, out_sems
):
    fetches = [pltpu.make_async_copy(halfway.at[b], held.at[b], sems.at[b]) for b in range(RIGHT)]
    for copy in fetches:
        copy.start()
    half = ROWS // 2
    statistics = [
        unpacked(gathered[s * half : (s + 1) * half, PACK:, :].reshape(BLOCK, HALF), diagonals[1 + s : 2 + s, :])
        for s in range(2)
    ]
    found = []
    chain = root_steps(statistics, found)
    copies = []

    def stored(b, start, size, sem):
        rows = pl.ds(start, size)
        copy = pltpu.make_async_copy(
            buffer.at[b, rows], out.at[rows, pl.ds(b * BLOCK, BLOCK)], out_sems.at[sem]
        )
        copy.start()
        copies.append(copy)

    for _ in range(7):
        next(chain)
    for copy in fetches:
        copy.wait()
    for b in range(RIGHT - 1):
        one, two = [parts(unpacked(gathered[2 * b + s, :PACK, :])) for s in range(2)]
        for _ in applied(held, b, one, two, buffer):
            next(chain)
        stored(b, 0, 2 * BLOCK, b)
    for _ in chain:
        pass
    last = RIGHT - 1
    for k, _ in enumerate(applied(held, last, parts(found[0]), parts(found[1]), buffer)):
        stored(last, k * BLOCK, BLOCK, last + k)
    for copy in copies:
        copy.wait()


VMEM = pl.BlockSpec(memory_space=pltpu.VMEM)
SMEM = pl.BlockSpec(memory_space=pltpu.SMEM)
HBM = pl.BlockSpec(memory_space=pltpu.HBM)


def in_hbm(*values):
    return [pltpu.with_memory_space_constraint(value, pltpu.HBM) for value in values]


def params():
    return pltpu.CompilerParams(vmem_limit_bytes=32 * 1024 * 1024)


def cost(flops, moved):
    return pl.CostEstimate(flops=int(flops), bytes_accessed=int(moved), transcendentals=0)


def body(grad_first, grad_second):
    rows, cols = grad_first.shape
    col = lax.axis_index("col")
    core = lax.rem(col, 2)
    low_y = lax.rem(col // 4, 2)
    info = core.reshape(1).astype(jnp.int32)
    pair = jax.ShapeDtypeStruct((2 * PACK, HALF), f32)
    single = jax.ShapeDtypeStruct((PACK, HALF), f32)
    grads = 2 * rows * cols * 4
    passes = 3 * 2 * BLOCK * rows * cols * 2
    newton = 20 * 6 * BLOCK**3
    tiles = [pltpu.VMEM((2, RIGHT, rows, BLOCK), f32)]
    tile_sems = [pltpu.SemaphoreType.DMA((2, RIGHT))]

    right_parts = pl.pallas_call(
        right_stats_kernel,
        in_specs=[HBM, HBM],
        out_specs=HBM,
        out_shape=pltpu.HBM((ROWS, SLOT, HALF), f32),
        scratch_shapes=tiles
        + [pltpu.VMEM((ROWS, SLOT, HALF), f32)]
        + tile_sems
        + [pltpu.SemaphoreType.DMA((RIGHT - 1,))],
        compiler_params=params(),
        cost_estimate=cost(passes, grads),
        name="right_stats",
    )(*in_hbm(grad_first, grad_second))
    arrived = exchanged(right_parts)

    info, right_parts = lax.optimization_barrier((info, right_parts))
    keep, send = pl.pallas_call(
        left_stats_kernel,
        in_specs=[SMEM, HBM, HBM],
        out_specs=[VMEM, VMEM],
        out_shape=[pair, pair],
        scratch_shapes=tiles + [pltpu.VMEM((2, 2, BLOCK, 2 * BLOCK), f32)] + tile_sems,
        compiler_params=params(),
        cost_estimate=cost(passes, grads),
        name="left_stats",
    )(info, *in_hbm(grad_first, grad_second))
    both = (keep + swap(send, 1)).reshape(2, PACK, HALF)
    own = lax.dynamic_index_in_dim(both, low_y, 0, keepdims=False)
    rest = lax.dynamic_index_in_dim(both, 1 - low_y, 0, keepdims=False)
    own = (own + swap(rest, 4)) + (swap(own, 8) + swap(rest, 12))
    left_in = [own, swap(own, 2)]
    own, arrived = lax.optimization_barrier((own, arrived))

    right_root, diagonals = pl.pallas_call(
        right_roots_kernel,
        in_specs=[VMEM],
        out_specs=[VMEM, VMEM],
        out_shape=[jax.ShapeDtypeStruct((ROWS, SLOT, HALF), f32), jax.ShapeDtypeStruct((8, HALF), f32)],
        compiler_params=params(),
        cost_estimate=cost(newton, 2 * ROWS * SLOT * HALF * 4),
        name="right_roots",
    )(arrived)
    left_in, right_root = lax.optimization_barrier((left_in, right_root))
    gathered = exchanged(right_root)
    left_in, right_root = lax.optimization_barrier((left_in, right_root))
    left_root = pl.pallas_call(
        left_root_kernel,
        in_specs=[VMEM, VMEM],
        out_specs=VMEM,
        out_shape=single,
        compiler_params=params(),
        cost_estimate=cost(newton, 3 * PACK * HALF * 4),
        name="left_root",
    )(*left_in)
    left_other = swap(left_root, 4)
    mine = jnp.where(
        low_y == 0,
        jnp.concatenate([left_root, left_other]),
        jnp.concatenate([left_other, left_root]),
    )
    other = swap(mine, 1)

    held = (RIGHT, 4, rows, BLOCK)
    tile_sem = pltpu.SemaphoreType.DMA((RIGHT,))
    halfway = pl.pallas_call(
        halfway_kernel,
        in_specs=[SMEM, HBM, HBM, VMEM, VMEM],
        out_specs=HBM,
        out_shape=pltpu.HBM(held, bf16),
        scratch_shapes=tiles + [pltpu.VMEM(held, bf16)] + tile_sems + [tile_sem],
        compiler_params=params(),
        cost_estimate=cost(passes, 2 * grads),
        name="halfway",
    )(info, *in_hbm(grad_first, grad_second), mine, other)

    return pl.pallas_call(
        finish_kernel,
        in_specs=[HBM, VMEM, VMEM],
        out_specs=HBM,
        scratch_shapes=[
            pltpu.VMEM(held, bf16),
            pltpu.VMEM((RIGHT, rows, BLOCK), f32),
            tile_sem,
            pltpu.SemaphoreType.DMA((RIGHT + 1,)),
        ],
        out_shape=jax.ShapeDtypeStruct((rows, cols), f32),
        compiler_params=params(),
        cost_estimate=cost(passes + 2 * newton, 2 * grads),
        name="finish",
    )(*in_hbm(halfway), gathered, diagonals)


def solution(mesh):
    in_specs = (P("row", "col"), P("row", "col"))
    out_specs = P("row", "col")
    return jax.shard_map(body, mesh=mesh, in_specs=in_specs, out_specs=out_specs, check_vma=False)
```

```python
import jax
import jax.numpy as jnp
from jax import lax
from jax.experimental import pallas as pl
from jax.experimental.pallas import tpu as pltpu
from jax.sharding import PartitionSpec as P

D = 4096
FF = 20480
BLOCK = 256
HALF = 128
ITERS = 6
DAMPING = 0.001
ROWS = 8
COLS = 16
RIGHT = 5
SHARE = 2 * BLOCK // ROWS
SLOT = BLOCK + 8 + SHARE
PACK = BLOCK + 8

f32 = jnp.float32
bf16 = jnp.bfloat16

def swap(value, d):
    return lax.ppermute(value, "col", [(i, i ^ d) for i in range(COLS)])


def exchanged(slots):
    return lax.all_to_all(slots, "row", split_axis=0, concat_axis=0, tiled=True)


def parts(value):
    high = value.astype(bf16)
    return high, (value - high.astype(f32)).astype(bf16)


def dot(left, right, dims=((1,), (0,))):
    return lax.dot_general(left, right, (dims, ((), ())), preferred_element_type=f32)


def product(left, right):
    (lh, ll), (rh, rl) = left, right
    return dot(lh, rh) + (dot(lh, rl) + dot(ll, rh))


def halves_product(left, right):
    return jnp.concatenate(
        [product([part[k : k + HALF] for part in left], right) for k in (0, HALF)], axis=0
    )


def iotas(n):
    return (
        lax.broadcasted_iota(jnp.int32, (n, n), 0),
        lax.broadcasted_iota(jnp.int32, (n, n), 1),
    )


def packed_parts(block):
    i, j = iotas(HALF)
    first, last = block[:HALF, :HALF], block[HALF:, HALF:]
    quarters = jnp.concatenate([block[:HALF, HALF:], jnp.where(i >= j, first, last)], axis=0)
    return quarters, jnp.sum(jnp.where(i == j, last, 0.0), axis=0, keepdims=True)


def packed_gram(even, odd):
    i, j = iotas(HALF)
    first, last = odd[:HALF, :HALF], odd[HALF:, HALF:]
    upper = even[:HALF, HALF:] + odd[:HALF, HALF:] + odd[HALF:, :HALF].T
    mixed = jnp.where(i >= j, even[:HALF, :HALF] + first, even[HALF:, HALF:] + last)
    mixed = mixed + jnp.where(i <= j, first, last).T
    diagonal = jnp.sum(jnp.where(i == j, even[HALF:, HALF:] + 2.0 * last, 0.0), axis=0, keepdims=True)
    return jnp.concatenate([upper, mixed], axis=0), diagonal


def store_packed(ref, start, block):
    quarters, diagonal = packed_parts(block)
    ref[pl.ds(start, BLOCK), :] = quarters
    ref[pl.ds(start + BLOCK, 8), :] = jnp.broadcast_to(diagonal, (8, HALF))


def unpacked(packed, diagonal=None):
    i, j = iotas(HALF)
    upper, mixed = packed[:HALF], packed[HALF:BLOCK]
    if diagonal is None:
        diagonal = packed[BLOCK : BLOCK + 1]
    turned = mixed.T
    first = jnp.where(i >= j, mixed, turned)
    last = jnp.where(i < j, mixed, jnp.where(i == j, jnp.broadcast_to(diagonal, (HALF, HALF)), turned))
    return jnp.concatenate(
        [
            jnp.concatenate([first, upper], axis=1),
            jnp.concatenate([upper.T, last], axis=1),
        ],
        axis=0,
    )


def root_steps(statistics, found):
    i, j = iotas(BLOCK)
    identity = jnp.where(i == j, 1.0, 0.0).astype(f32)
    currents, scaleds, squares = [], [], []
    for statistic in statistics:
        damped = statistic + DAMPING * identity
        split = parts(damped)
        square = halves_product(split, split)
        norm = jnp.sqrt(jnp.sum(damped * damped, axis=(0, 1), keepdims=True))
        inverse = 1.0 / norm
        scaled = damped * inverse
        currents.append(lax.rsqrt(jnp.sqrt(norm)))
        scaleds.append(scaled)
        squares.append(
            parts((25.0 / 16.0) * identity - (10.0 / 16.0) * scaled + (square * inverse) * (inverse * (1.0 / 16.0)))
        )
    yield
    for iteration in range(ITERS):
        factors = [(5.0 * identity - scaled) * 0.25 for scaled in scaleds]
        split = [parts(factor) for factor in factors]
        if iteration == ITERS - 1:
            found.extend(halves_product(parts(current), fs) for current, fs in zip(currents, split))
            return
        if iteration == 0:
            currents = [current * factor for current, factor in zip(currents, factors)]
        else:
            squares = [parts(halves_product(fs, fs)) for fs in split]
            yield
            currents = [halves_product(parts(current), fs) for current, fs in zip(currents, split)]
        fourths = [parts(halves_product(sq, sq)) for sq in squares]
        yield
        scaleds = [halves_product(fo, parts(scaled)) for fo, scaled in zip(fourths, scaleds)]
        yield


def roots(statistics):
    found = []
    for _ in root_steps(statistics, found):
        pass
    return found


def fetched(sources, buffer, sems, order=range(RIGHT)):
    tiles = {}
    for b in order:
        columns = pl.ds(b * BLOCK, BLOCK)
        tiles[b] = [
            pltpu.make_async_copy(source.at[:, columns], buffer.at[s, b], sems.at[s, b])
            for s, source in enumerate(sources)
        ]
        for copy in tiles[b]:
            copy.start()
    return tiles


def right_stats_kernel(first, second, out, buffer, slots, sems, out_sems):
    groups = ((RIGHT - 1,), (0, 1), (2, 3))
    tiles = fetched((first, second), buffer, sems, sum(groups, ()))
    half = ROWS // 2
    copies = []
    for slot in range(ROWS):
        slots[slot, BLOCK + 3 : BLOCK + 8, :] = jnp.zeros((5, HALF), f32)
    for group in groups:
        for b in group:
            for copy in tiles[b]:
                copy.wait()
        packed = []
        for b in group:
            for s in range(2):
                high, low = parts(buffer[s, b])
                gram = dot(high, jnp.concatenate([high, low], axis=1), ((0,), (0,))) * (1.0 / D)
                packed.append(packed_gram(gram[:, :BLOCK], gram[:, BLOCK:]))
        for k, b in enumerate(group):
            one, two = packed[2 * k : 2 * k + 2]
            for s, (quarters, diagonal) in enumerate((one, (one[0] + two[0], one[1] + two[1]))):
                if b < RIGHT - 1:
                    slots[2 * b + s, :BLOCK, :] = quarters
                    slots[2 * b + s, BLOCK : BLOCK + 1, :] = diagonal
                else:
                    slots[s * half : (s + 1) * half, BLOCK + 8 :, :] = quarters.reshape(half, SHARE, HALF)
                    for slot in range(ROWS):
                        slots[slot, BLOCK + 1 + s : BLOCK + 2 + s, :] = diagonal
        for b in group:
            if b < RIGHT - 1:
                pair = pl.ds(2 * b, 2)
                copies.append(pltpu.make_async_copy(slots.at[pair], out.at[pair], out_sems.at[b]))
                copies[-1].start()
    for copy in copies:
        copy.wait()


def left_stats_kernel(info, first, second, keep, send, buffer, sums, sems):
    core = info[0]
    tiles = fetched((first, second), buffer, sems)
    for b in range(RIGHT):
        for copy in tiles[b]:
            copy.wait()
        for s in range(2):
            for block in range(2):
                high, low = parts(buffer[s, b, block * BLOCK : (block + 1) * BLOCK, :])
                gram = dot(high, jnp.concatenate([high, low], axis=0), ((1,), (1,)))
                if b == 0:
                    sums[block, s] = gram
                else:
                    sums[block, s] += gram
    for out, block in ((keep, core), (send, 1 - core)):
        total = None
        for s in range(2):
            gram = sums[block, s] * (1.0 / FF)
            gram = packed_gram(gram[:, :BLOCK], gram[:, BLOCK:])
            total = gram if s == 0 else (total[0] + gram[0], total[1] + gram[1])
            out[s * PACK : s * PACK + BLOCK, :] = total[0]
            out[s * PACK + BLOCK : (s + 1) * PACK, :] = jnp.broadcast_to(total[1], (8, HALF))


def right_roots_kernel(arrived, right_out, diagonals):
    total = arrived[0]
    for slot in range(1, ROWS):
        total = total + arrived[slot]
    for slot in range(ROWS):
        right_out[slot, PACK:, :] = total[PACK:]
    diagonals[...] = total[BLOCK:PACK]
    (root,) = roots([unpacked(total[:PACK])])
    quarters, diagonal = packed_parts(root)
    for slot in range(ROWS):
        right_out[slot, :BLOCK, :] = quarters
        right_out[slot, BLOCK:PACK, :] = jnp.broadcast_to(diagonal, (8, HALF))


def left_root_kernel(own, other, out):
    (root,) = roots([unpacked(own[...] + other[...])])
    store_packed(out, 0, root)


def halfway_kernel(info, first, second, mine, other, out, buffer, results, sems, out_sems):
    core = info[0]
    tiles = fetched((first, second), buffer, sems)
    split = [[parts(unpacked(ref[s * PACK : (s + 1) * PACK, :])) for s in range(2)] for ref in (mine, other)]
    copies = []
    for b in range(RIGHT):
        for copy in tiles[b]:
            copy.wait()
        for s in range(2):
            for place, block in enumerate((core, 1 - core)):
                rows = pl.ds(pl.multiple_of(block * BLOCK, BLOCK), BLOCK)
                result = product(split[place][s], parts(buffer[s, b, rows, :]))
                results[b, 2 * s, rows, :], results[b, 2 * s + 1, rows, :] = parts(result)
        copy = pltpu.make_async_copy(results.at[b], out.at[b], out_sems.at[b])
        copy.start()
        copies.append(copy)
    for copy in copies:
        copy.wait()


def applied(held, b, one, two, buffer):
    (h1, l1), (h2, l2) = one, two
    weights = jnp.concatenate([h1, h1, l1, h2, h2, l2], axis=0)
    for start in (0, BLOCK):
        rows = slice(start, start + BLOCK)
        high_one, low_one, high_two, low_two = [held[b, q, rows, :] for q in range(4)]
        lhs = jnp.concatenate([low_one, high_one, high_one, low_two, high_two, high_two], axis=1)
        buffer[b, rows, :] = dot(lhs, weights)
        yield


def finish_kernel(
    halfway, gathered, diagonals, out, held, buffer, sems, out_sems
):
    fetches = [pltpu.make_async_copy(halfway.at[b], held.at[b], sems.at[b]) for b in range(RIGHT)]
    for copy in fetches:
        copy.start()
    half = ROWS // 2
    statistics = [
        unpacked(gathered[s * half : (s + 1) * half, PACK:, :].reshape(BLOCK, HALF), diagonals[1 + s : 2 + s, :])
        for s in range(2)
    ]
    found = []
    chain = root_steps(statistics, found)
    copies = []

    def stored(b, start, size, sem):
        rows = pl.ds(start, size)
        copy = pltpu.make_async_copy(
            buffer.at[b, rows], out.at[rows, pl.ds(b * BLOCK, BLOCK)], out_sems.at[sem]
        )
        copy.start()
        copies.append(copy)

    for _ in range(7):
        next(chain)
    for copy in fetches:
        copy.wait()
    for b in range(RIGHT - 1):
        one, two = [parts(unpacked(gathered[2 * b + s, :PACK, :])) for s in range(2)]
        for _ in applied(held, b, one, two, buffer):
            next(chain)
        stored(b, 0, 2 * BLOCK, b)
    for _ in chain:
        pass
    last = RIGHT - 1
    for k, _ in enumerate(applied(held, last, parts(found[0]), parts(found[1]), buffer)):
        stored(last, k * BLOCK, BLOCK, last + k)
    for copy in copies:
        copy.wait()


VMEM = pl.BlockSpec(memory_space=pltpu.VMEM)
SMEM = pl.BlockSpec(memory_space=pltpu.SMEM)
HBM = pl.BlockSpec(memory_space=pltpu.HBM)


def in_hbm(*values):
    return [pltpu.with_memory_space_constraint(value, pltpu.HBM) for value in values]


def params():
    return pltpu.CompilerParams(vmem_limit_bytes=32 * 1024 * 1024)


def cost(flops, moved):
    return pl.CostEstimate(flops=int(flops), bytes_accessed=int(moved), transcendentals=0)


def body(grad_first, grad_second):
    rows, cols = grad_first.shape
    col = lax.axis_index("col")
    core = lax.rem(col, 2)
    low_y = lax.rem(col // 4, 2)
    info = core.reshape(1).astype(jnp.int32)
    pair = jax.ShapeDtypeStruct((2 * PACK, HALF), f32)
    single = jax.ShapeDtypeStruct((PACK, HALF), f32)
    grads = 2 * rows * cols * 4
    passes = 3 * 2 * BLOCK * rows * cols * 2
    newton = 20 * 6 * BLOCK**3
    tiles = [pltpu.VMEM((2, RIGHT, rows, BLOCK), f32)]
    tile_sems = [pltpu.SemaphoreType.DMA((2, RIGHT))]

    right_parts = pl.pallas_call(
        right_stats_kernel,
        in_specs=[HBM, HBM],
        out_specs=HBM,
        out_shape=pltpu.HBM((ROWS, SLOT, HALF), f32),
        scratch_shapes=tiles
        + [pltpu.VMEM((ROWS, SLOT, HALF), f32)]
        + tile_sems
        + [pltpu.SemaphoreType.DMA((RIGHT - 1,))],
        compiler_params=params(),
        cost_estimate=cost(passes, grads),
        name="right_stats",
    )(*in_hbm(grad_first, grad_second))
    arrived = exchanged(right_parts)

    info, right_parts = lax.optimization_barrier((info, right_parts))
    keep, send = pl.pallas_call(
        left_stats_kernel,
        in_specs=[SMEM, HBM, HBM],
        out_specs=[VMEM, VMEM],
        out_shape=[pair, pair],
        scratch_shapes=tiles + [pltpu.VMEM((2, 2, BLOCK, 2 * BLOCK), f32)] + tile_sems,
        compiler_params=params(),
        cost_estimate=cost(passes, grads),
        name="left_stats",
    )(info, *in_hbm(grad_first, grad_second))
    both = (keep + swap(send, 1)).reshape(2, PACK, HALF)
    own = lax.dynamic_index_in_dim(both, low_y, 0, keepdims=False)
    rest = lax.dynamic_index_in_dim(both, 1 - low_y, 0, keepdims=False)
    own = (own + swap(rest, 4)) + (swap(own, 8) + swap(rest, 12))
    left_in = [own, swap(own, 2)]
    own, arrived = lax.optimization_barrier((own, arrived))

    right_root, diagonals = pl.pallas_call(
        right_roots_kernel,
        in_specs=[VMEM],
        out_specs=[VMEM, VMEM],
        out_shape=[jax.ShapeDtypeStruct((ROWS, SLOT, HALF), f32), jax.ShapeDtypeStruct((8, HALF), f32)],
        compiler_params=params(),
        cost_estimate=cost(newton, 2 * ROWS * SLOT * HALF * 4),
        name="right_roots",
    )(arrived)
    left_in, right_root = lax.optimization_barrier((left_in, right_root))
    gathered = exchanged(right_root)
    left_in, right_root = lax.optimization_barrier((left_in, right_root))
    left_root = pl.pallas_call(
        left_root_kernel,
        in_specs=[VMEM, VMEM],
        out_specs=VMEM,
        out_shape=single,
        compiler_params=params(),
        cost_estimate=cost(newton, 3 * PACK * HALF * 4),
        name="left_root",
    )(*left_in)
    def ordered(own_step, other_step):
        return jnp.where(
            low_y == 0,
            jnp.concatenate([own_step, other_step]),
            jnp.concatenate([other_step, own_step]),
        )

    from_y, from_core, from_both = swap(left_root, 4), swap(left_root, 1), swap(left_root, 5)
    mine, other = ordered(left_root, from_y), ordered(from_core, from_both)

    held = (RIGHT, 4, rows, BLOCK)
    tile_sem = pltpu.SemaphoreType.DMA((RIGHT,))
    halfway = pl.pallas_call(
        halfway_kernel,
        in_specs=[SMEM, HBM, HBM, VMEM, VMEM],
        out_specs=HBM,
        out_shape=pltpu.HBM(held, bf16),
        scratch_shapes=tiles + [pltpu.VMEM(held, bf16)] + tile_sems + [tile_sem],
        compiler_params=params(),
        cost_estimate=cost(passes, 2 * grads),
        name="halfway",
    )(info, *in_hbm(grad_first, grad_second), mine, other)

    return pl.pallas_call(
        finish_kernel,
        in_specs=[HBM, VMEM, VMEM],
        out_specs=HBM,
        scratch_shapes=[
            pltpu.VMEM(held, bf16),
            pltpu.VMEM((RIGHT, rows, BLOCK), f32),
            tile_sem,
            pltpu.SemaphoreType.DMA((RIGHT + 1,)),
        ],
        out_shape=jax.ShapeDtypeStruct((rows, cols), f32),
        compiler_params=params(),
        cost_estimate=cost(passes + 2 * newton, 2 * grads),
        name="finish",
    )(*in_hbm(halfway), gathered, diagonals)


def solution(mesh):
    in_specs = (P("row", "col"), P("row", "col"))
    out_specs = P("row", "col")
    return jax.shard_map(body, mesh=mesh, in_specs=in_specs, out_specs=out_specs, check_vma=False)
```

```python
import jax
import jax.numpy as jnp
from jax import lax
from jax.experimental import pallas as pl
from jax.experimental.pallas import tpu as pltpu
from jax.sharding import PartitionSpec as P

D = 4096
FF = 20480
BLOCK = 256
HALF = 128
ITERS = 6
DAMPING = 0.001
ROWS = 8
COLS = 16
RIGHT = 5
SHARE = 2 * BLOCK // ROWS
SLOT = BLOCK + 8 + SHARE
PACK = BLOCK + 8

f32 = jnp.float32
bf16 = jnp.bfloat16

def swap(value, d):
    return lax.ppermute(value, "col", [(i, i ^ d) for i in range(COLS)])


def exchanged(slots):
    return lax.all_to_all(slots, "row", split_axis=0, concat_axis=0, tiled=True)


def parts(value):
    high = value.astype(bf16)
    return high, (value - high.astype(f32)).astype(bf16)


def dot(left, right, dims=((1,), (0,))):
    return lax.dot_general(left, right, (dims, ((), ())), preferred_element_type=f32)


def product(left, right):
    (lh, ll), (rh, rl) = left, right
    return dot(lh, rh) + (dot(lh, rl) + dot(ll, rh))


def halves_product(left, right):
    return jnp.concatenate(
        [product([part[k : k + HALF] for part in left], right) for k in (0, HALF)], axis=0
    )


def iotas(n):
    return (
        lax.broadcasted_iota(jnp.int32, (n, n), 0),
        lax.broadcasted_iota(jnp.int32, (n, n), 1),
    )


def packed_parts(block):
    i, j = iotas(HALF)
    first, last = block[:HALF, :HALF], block[HALF:, HALF:]
    quarters = jnp.concatenate([block[:HALF, HALF:], jnp.where(i >= j, first, last)], axis=0)
    return quarters, jnp.sum(jnp.where(i == j, last, 0.0), axis=0, keepdims=True)


def packed_gram(even, odd):
    i, j = iotas(HALF)
    first, last = odd[:HALF, :HALF], odd[HALF:, HALF:]
    upper = even[:HALF, HALF:] + odd[:HALF, HALF:] + odd[HALF:, :HALF].T
    mixed = jnp.where(i >= j, even[:HALF, :HALF] + first, even[HALF:, HALF:] + last)
    mixed = mixed + jnp.where(i <= j, first, last).T
    diagonal = jnp.sum(jnp.where(i == j, even[HALF:, HALF:] + 2.0 * last, 0.0), axis=0, keepdims=True)
    return jnp.concatenate([upper, mixed], axis=0), diagonal


def store_packed(ref, start, block):
    quarters, diagonal = packed_parts(block)
    ref[pl.ds(start, BLOCK), :] = quarters
    ref[pl.ds(start + BLOCK, 8), :] = jnp.broadcast_to(diagonal, (8, HALF))


def unpacked(packed, diagonal=None):
    i, j = iotas(HALF)
    upper, mixed = packed[:HALF], packed[HALF:BLOCK]
    if diagonal is None:
        diagonal = packed[BLOCK : BLOCK + 1]
    turned = mixed.T
    first = jnp.where(i >= j, mixed, turned)
    last = jnp.where(i < j, mixed, jnp.where(i == j, jnp.broadcast_to(diagonal, (HALF, HALF)), turned))
    return jnp.concatenate(
        [
            jnp.concatenate([first, upper], axis=1),
            jnp.concatenate([upper.T, last], axis=1),
        ],
        axis=0,
    )


def root_steps(statistics, found):
    i, j = iotas(BLOCK)
    identity = jnp.where(i == j, 1.0, 0.0).astype(f32)
    currents, scaleds, squares = [], [], []
    for statistic in statistics:
        damped = statistic + DAMPING * identity
        split = parts(damped)
        square = halves_product(split, split)
        norm = jnp.sqrt(jnp.sum(damped * damped, axis=(0, 1), keepdims=True))
        inverse = 1.0 / norm
        scaled = damped * inverse
        currents.append(lax.rsqrt(jnp.sqrt(norm)))
        scaleds.append(scaled)
        squares.append(
            parts((25.0 / 16.0) * identity - (10.0 / 16.0) * scaled + (square * inverse) * (inverse * (1.0 / 16.0)))
        )
    yield
    for iteration in range(ITERS):
        factors = [(5.0 * identity - scaled) * 0.25 for scaled in scaleds]
        split = [parts(factor) for factor in factors]
        if iteration == ITERS - 1:
            found.extend(halves_product(parts(current), fs) for current, fs in zip(currents, split))
            return
        if iteration == 0:
            currents = [current * factor for current, factor in zip(currents, factors)]
        else:
            squares = [parts(halves_product(fs, fs)) for fs in split]
            yield
            currents = [halves_product(parts(current), fs) for current, fs in zip(currents, split)]
        fourths = [parts(halves_product(sq, sq)) for sq in squares]
        yield
        scaleds = [halves_product(fo, parts(scaled)) for fo, scaled in zip(fourths, scaleds)]
        yield


def roots(statistics):
    found = []
    for _ in root_steps(statistics, found):
        pass
    return found


def fetched(sources, buffer, sems, order=range(RIGHT)):
    tiles = {}
    for b in order:
        columns = pl.ds(b * BLOCK, BLOCK)
        tiles[b] = [
            pltpu.make_async_copy(source.at[:, columns], buffer.at[s, b], sems.at[s, b])
            for s, source in enumerate(sources)
        ]
        for copy in tiles[b]:
            copy.start()
    return tiles


def right_stats_kernel(first, second, out, buffer, slots, sems, out_sems):
    groups = ((RIGHT - 1,), (0, 1), (2, 3))
    tiles = fetched((first, second), buffer, sems, sum(groups, ()))
    half = ROWS // 2
    copies = []
    for slot in range(ROWS):
        slots[slot, BLOCK + 3 : BLOCK + 8, :] = jnp.zeros((5, HALF), f32)
    for group in groups:
        for b in group:
            for copy in tiles[b]:
                copy.wait()
        packed = []
        for b in group:
            for s in range(2):
                high, low = parts(buffer[s, b])
                gram = dot(high, jnp.concatenate([high, low], axis=1), ((0,), (0,))) * (1.0 / D)
                packed.append(packed_gram(gram[:, :BLOCK], gram[:, BLOCK:]))
        for k, b in enumerate(group):
            one, two = packed[2 * k : 2 * k + 2]
            for s, (quarters, diagonal) in enumerate((one, (one[0] + two[0], one[1] + two[1]))):
                if b < RIGHT - 1:
                    slots[2 * b + s, :BLOCK, :] = quarters
                    slots[2 * b + s, BLOCK : BLOCK + 1, :] = diagonal
                else:
                    slots[s * half : (s + 1) * half, BLOCK + 8 :, :] = quarters.reshape(half, SHARE, HALF)
                    for slot in range(ROWS):
                        slots[slot, BLOCK + 1 + s : BLOCK + 2 + s, :] = diagonal
        for b in group:
            if b < RIGHT - 1:
                pair = pl.ds(2 * b, 2)
                copies.append(pltpu.make_async_copy(slots.at[pair], out.at[pair], out_sems.at[b]))
                copies[-1].start()
    for copy in copies:
        copy.wait()


def left_stats_kernel(info, first, second, keep, send, buffer, sums, sems):
    core = info[0]
    tiles = fetched((first, second), buffer, sems)
    for b in range(RIGHT):
        for copy in tiles[b]:
            copy.wait()
        for s in range(2):
            for block in range(2):
                high, low = parts(buffer[s, b, block * BLOCK : (block + 1) * BLOCK, :])
                gram = dot(high, jnp.concatenate([high, low], axis=0), ((1,), (1,)))
                if b == 0:
                    sums[block, s] = gram
                else:
                    sums[block, s] += gram
    for out, block in ((keep, core), (send, 1 - core)):
        total = None
        for s in range(2):
            gram = sums[block, s] * (1.0 / FF)
            gram = packed_gram(gram[:, :BLOCK], gram[:, BLOCK:])
            total = gram if s == 0 else (total[0] + gram[0], total[1] + gram[1])
            out[s * PACK : s * PACK + BLOCK, :] = total[0]
            out[s * PACK + BLOCK : (s + 1) * PACK, :] = jnp.broadcast_to(total[1], (8, HALF))


def right_roots_kernel(arrived, right_out, diagonals):
    total = arrived[0]
    for slot in range(1, ROWS):
        total = total + arrived[slot]
    for slot in range(ROWS):
        right_out[slot, PACK:, :] = total[PACK:]
    diagonals[...] = total[BLOCK:PACK]
    (root,) = roots([unpacked(total[:PACK])])
    quarters, diagonal = packed_parts(root)
    for slot in range(ROWS):
        right_out[slot, :BLOCK, :] = quarters
        right_out[slot, BLOCK:PACK, :] = jnp.broadcast_to(diagonal, (8, HALF))


def left_root_kernel(own, other, out):
    (root,) = roots([unpacked(own[...] + other[...])])
    store_packed(out, 0, root)


def halfway_kernel(info, first, second, mine, other, out, buffer, results, sems, out_sems):
    core = info[0]
    tiles = fetched((first, second), buffer, sems)
    split = [[parts(unpacked(ref[s * PACK : (s + 1) * PACK, :])) for s in range(2)] for ref in (mine, other)]
    copies = []
    for b in range(RIGHT):
        for copy in tiles[b]:
            copy.wait()
        for s in range(2):
            for place, block in enumerate((core, 1 - core)):
                rows = pl.ds(pl.multiple_of(block * BLOCK, BLOCK), BLOCK)
                result = product(split[place][s], parts(buffer[s, b, rows, :]))
                results[b, 2 * s, rows, :], results[b, 2 * s + 1, rows, :] = parts(result)
        copy = pltpu.make_async_copy(results.at[b], out.at[b], out_sems.at[b])
        copy.start()
        copies.append(copy)
    for copy in copies:
        copy.wait()


def applied(held, b, one, two, buffer):
    (h1, l1), (h2, l2) = one, two
    weights = jnp.concatenate([h1, h1, l1, h2, h2, l2], axis=0)
    for start in (0, BLOCK):
        rows = slice(start, start + BLOCK)
        high_one, low_one, high_two, low_two = [held[b, q, rows, :] for q in range(4)]
        lhs = jnp.concatenate([low_one, high_one, high_one, low_two, high_two, high_two], axis=1)
        buffer[b, rows, :] = dot(lhs, weights)
        yield


def finish_kernel(
    halfway, gathered, diagonals, out, held, buffer, sems, out_sems
):
    fetches = [pltpu.make_async_copy(halfway.at[b], held.at[b], sems.at[b]) for b in range(RIGHT)]
    for copy in fetches:
        copy.start()
    half = ROWS // 2
    statistics = [
        unpacked(gathered[s * half : (s + 1) * half, PACK:, :].reshape(BLOCK, HALF), diagonals[1 + s : 2 + s, :])
        for s in range(2)
    ]
    found = []
    chain = root_steps(statistics, found)
    copies = []

    def stored(b, start, size, sem):
        rows = pl.ds(start, size)
        copy = pltpu.make_async_copy(
            buffer.at[b, rows], out.at[rows, pl.ds(b * BLOCK, BLOCK)], out_sems.at[sem]
        )
        copy.start()
        copies.append(copy)

    for _ in range(7):
        next(chain)
    for copy in fetches:
        copy.wait()
    for b in range(RIGHT - 1):
        one, two = [parts(unpacked(gathered[2 * b + s, :PACK, :])) for s in range(2)]
        for _ in applied(held, b, one, two, buffer):
            next(chain)
        stored(b, 0, 2 * BLOCK, b)
    for _ in chain:
        pass
    last = RIGHT - 1
    for k, _ in enumerate(applied(held, last, parts(found[0]), parts(found[1]), buffer)):
        stored(last, k * BLOCK, BLOCK, last + k)
    for copy in copies:
        copy.wait()


VMEM = pl.BlockSpec(memory_space=pltpu.VMEM)
SMEM = pl.BlockSpec(memory_space=pltpu.SMEM)
HBM = pl.BlockSpec(memory_space=pltpu.HBM)


def in_hbm(*values):
    return [pltpu.with_memory_space_constraint(value, pltpu.HBM) for value in values]


def params():
    return pltpu.CompilerParams(vmem_limit_bytes=32 * 1024 * 1024)


def cost(flops, moved):
    return pl.CostEstimate(flops=int(flops), bytes_accessed=int(moved), transcendentals=0)


def body(grad_first, grad_second):
    rows, cols = grad_first.shape
    col = lax.axis_index("col")
    core = lax.rem(col, 2)
    low_y = lax.rem(col // 4, 2)
    info = core.reshape(1).astype(jnp.int32)
    pair = jax.ShapeDtypeStruct((2 * PACK, HALF), f32)
    single = jax.ShapeDtypeStruct((PACK, HALF), f32)
    grads = 2 * rows * cols * 4
    passes = 3 * 2 * BLOCK * rows * cols * 2
    newton = 20 * 6 * BLOCK**3
    tiles = [pltpu.VMEM((2, RIGHT, rows, BLOCK), f32)]
    tile_sems = [pltpu.SemaphoreType.DMA((2, RIGHT))]

    right_parts = pl.pallas_call(
        right_stats_kernel,
        in_specs=[HBM, HBM],
        out_specs=HBM,
        out_shape=pltpu.HBM((ROWS, SLOT, HALF), f32),
        scratch_shapes=tiles
        + [pltpu.VMEM((ROWS, SLOT, HALF), f32)]
        + tile_sems
        + [pltpu.SemaphoreType.DMA((RIGHT - 1,))],
        compiler_params=params(),
        cost_estimate=cost(passes, grads),
        name="right_stats",
    )(*in_hbm(grad_first, grad_second))
    arrived = exchanged(right_parts)

    info, right_parts = lax.optimization_barrier((info, right_parts))
    keep, send = pl.pallas_call(
        left_stats_kernel,
        in_specs=[SMEM, HBM, HBM],
        out_specs=[VMEM, VMEM],
        out_shape=[pair, pair],
        scratch_shapes=tiles + [pltpu.VMEM((2, 2, BLOCK, 2 * BLOCK), f32)] + tile_sems,
        compiler_params=params(),
        cost_estimate=cost(passes, grads),
        name="left_stats",
    )(info, *in_hbm(grad_first, grad_second))
    both = (keep + swap(send, 1)).reshape(2, PACK, HALF)
    own = lax.dynamic_index_in_dim(both, low_y, 0, keepdims=False)
    rest = lax.dynamic_index_in_dim(both, 1 - low_y, 0, keepdims=False)
    own = (own + swap(own, 8)) + (swap(rest, 4) + swap(rest, 12))
    left_in = [own, swap(own, 2)]
    own, arrived = lax.optimization_barrier((own, arrived))

    right_root, diagonals = pl.pallas_call(
        right_roots_kernel,
        in_specs=[VMEM],
        out_specs=[VMEM, VMEM],
        out_shape=[jax.ShapeDtypeStruct((ROWS, SLOT, HALF), f32), jax.ShapeDtypeStruct((8, HALF), f32)],
        compiler_params=params(),
        cost_estimate=cost(newton, 2 * ROWS * SLOT * HALF * 4),
        name="right_roots",
    )(arrived)
    left_in, right_root = lax.optimization_barrier((left_in, right_root))
    gathered = exchanged(right_root)
    left_in, right_root = lax.optimization_barrier((left_in, right_root))
    left_root = pl.pallas_call(
        left_root_kernel,
        in_specs=[VMEM, VMEM],
        out_specs=VMEM,
        out_shape=single,
        compiler_params=params(),
        cost_estimate=cost(newton, 3 * PACK * HALF * 4),
        name="left_root",
    )(*left_in)
    left_other = swap(left_root, 4)
    mine = jnp.where(
        low_y == 0,
        jnp.concatenate([left_root, left_other]),
        jnp.concatenate([left_other, left_root]),
    )
    other = swap(mine, 1)

    held = (RIGHT, 4, rows, BLOCK)
    tile_sem = pltpu.SemaphoreType.DMA((RIGHT,))
    halfway = pl.pallas_call(
        halfway_kernel,
        in_specs=[SMEM, HBM, HBM, VMEM, VMEM],
        out_specs=HBM,
        out_shape=pltpu.HBM(held, bf16),
        scratch_shapes=tiles + [pltpu.VMEM(held, bf16)] + tile_sems + [tile_sem],
        compiler_params=params(),
        cost_estimate=cost(passes, 2 * grads),
        name="halfway",
    )(info, *in_hbm(grad_first, grad_second), mine, other)

    return pl.pallas_call(
        finish_kernel,
        in_specs=[HBM, VMEM, VMEM],
        out_specs=HBM,
        scratch_shapes=[
            pltpu.VMEM(held, bf16),
            pltpu.VMEM((RIGHT, rows, BLOCK), f32),
            tile_sem,
            pltpu.SemaphoreType.DMA((RIGHT + 1,)),
        ],
        out_shape=jax.ShapeDtypeStruct((rows, cols), f32),
        compiler_params=params(),
        cost_estimate=cost(passes + 2 * newton, 2 * grads),
        name="finish",
    )(*in_hbm(halfway), gathered, diagonals)


def solution(mesh):
    in_specs = (P("row", "col"), P("row", "col"))
    out_specs = P("row", "col")
    return jax.shard_map(body, mesh=mesh, in_specs=in_specs, out_specs=out_specs, check_vma=False)
```

```python
import jax
import jax.numpy as jnp
from jax import lax
from jax.experimental import pallas as pl
from jax.experimental.pallas import tpu as pltpu
from jax.sharding import PartitionSpec as P

D = 4096
FF = 20480
BLOCK = 256
HALF = 128
ITERS = 6
DAMPING = 0.001
ROWS = 8
COLS = 16
RIGHT = 5
SHARE = 2 * BLOCK // ROWS
SLOT = BLOCK + 8 + SHARE
PACK = BLOCK + 8

f32 = jnp.float32
bf16 = jnp.bfloat16

def swap(value, d):
    return lax.ppermute(value, "col", [(i, i ^ d) for i in range(COLS)])


def exchanged(slots):
    return lax.all_to_all(slots, "row", split_axis=0, concat_axis=0, tiled=True)


def parts(value):
    high = value.astype(bf16)
    return high, (value - high.astype(f32)).astype(bf16)


def dot(left, right, dims=((1,), (0,))):
    return lax.dot_general(left, right, (dims, ((), ())), preferred_element_type=f32)


def product(left, right):
    (lh, ll), (rh, rl) = left, right
    return dot(lh, rh) + (dot(lh, rl) + dot(ll, rh))


def halves_product(left, right):
    return jnp.concatenate(
        [product([part[k : k + HALF] for part in left], right) for k in (0, HALF)], axis=0
    )


def iotas(n):
    return (
        lax.broadcasted_iota(jnp.int32, (n, n), 0),
        lax.broadcasted_iota(jnp.int32, (n, n), 1),
    )


def packed_parts(block):
    i, j = iotas(HALF)
    first, last = block[:HALF, :HALF], block[HALF:, HALF:]
    quarters = jnp.concatenate([block[:HALF, HALF:], jnp.where(i >= j, first, last)], axis=0)
    return quarters, jnp.sum(jnp.where(i == j, last, 0.0), axis=0, keepdims=True)


def packed_gram(even, odd):
    i, j = iotas(HALF)
    first, last = odd[:HALF, :HALF], odd[HALF:, HALF:]
    upper = even[:HALF, HALF:] + odd[:HALF, HALF:] + odd[HALF:, :HALF].T
    mixed = jnp.where(i >= j, even[:HALF, :HALF] + first, even[HALF:, HALF:] + last)
    mixed = mixed + jnp.where(i <= j, first, last).T
    diagonal = jnp.sum(jnp.where(i == j, even[HALF:, HALF:] + 2.0 * last, 0.0), axis=0, keepdims=True)
    return jnp.concatenate([upper, mixed], axis=0), diagonal


def store_packed(ref, start, block):
    quarters, diagonal = packed_parts(block)
    ref[pl.ds(start, BLOCK), :] = quarters
    ref[pl.ds(start + BLOCK, 8), :] = jnp.broadcast_to(diagonal, (8, HALF))


def unpacked(packed, diagonal=None):
    i, j = iotas(HALF)
    upper, mixed = packed[:HALF], packed[HALF:BLOCK]
    if diagonal is None:
        diagonal = packed[BLOCK : BLOCK + 1]
    turned = mixed.T
    first = jnp.where(i >= j, mixed, turned)
    last = jnp.where(i < j, mixed, jnp.where(i == j, jnp.broadcast_to(diagonal, (HALF, HALF)), turned))
    return jnp.concatenate(
        [
            jnp.concatenate([first, upper], axis=1),
            jnp.concatenate([upper.T, last], axis=1),
        ],
        axis=0,
    )


def root_steps(statistics, found):
    i, j = iotas(BLOCK)
    identity = jnp.where(i == j, 1.0, 0.0).astype(f32)
    currents, scaleds, squares = [], [], []
    for statistic in statistics:
        damped = statistic + DAMPING * identity
        split = parts(damped)
        square = halves_product(split, split)
        norm = jnp.sqrt(jnp.sum(damped * damped, axis=(0, 1), keepdims=True))
        inverse = 1.0 / norm
        scaled = damped * inverse
        currents.append(lax.rsqrt(jnp.sqrt(norm)))
        scaleds.append(scaled)
        squares.append(
            parts((25.0 / 16.0) * identity - (10.0 / 16.0) * scaled + (square * inverse) * (inverse * (1.0 / 16.0)))
        )
    yield
    for iteration in range(ITERS):
        factors = [(5.0 * identity - scaled) * 0.25 for scaled in scaleds]
        split = [parts(factor) for factor in factors]
        if iteration == ITERS - 1:
            found.extend(halves_product(parts(current), fs) for current, fs in zip(currents, split))
            return
        if iteration == 0:
            currents = [current * factor for current, factor in zip(currents, factors)]
        else:
            squares = [parts(halves_product(fs, fs)) for fs in split]
            yield
            currents = [halves_product(parts(current), fs) for current, fs in zip(currents, split)]
        fourths = [parts(halves_product(sq, sq)) for sq in squares]
        yield
        scaleds = [halves_product(fo, parts(scaled)) for fo, scaled in zip(fourths, scaleds)]
        yield


def roots(statistics):
    found = []
    for _ in root_steps(statistics, found):
        pass
    return found


def fetched(sources, buffer, sems, order=range(RIGHT)):
    tiles = {}
    for b in order:
        columns = pl.ds(b * BLOCK, BLOCK)
        tiles[b] = [
            pltpu.make_async_copy(source.at[:, columns], buffer.at[s, b], sems.at[s, b])
            for s, source in enumerate(sources)
        ]
        for copy in tiles[b]:
            copy.start()
    return tiles


def right_stats_kernel(first, second, out, buffer, slots, sems, out_sems):
    groups = ((RIGHT - 1,), (0, 1), (2, 3))
    tiles = fetched((first, second), buffer, sems, sum(groups, ()))
    half = ROWS // 2
    copies = []
    for slot in range(ROWS):
        slots[slot, BLOCK + 3 : BLOCK + 8, :] = jnp.zeros((5, HALF), f32)
    for group in groups:
        for b in group:
            for copy in tiles[b]:
                copy.wait()
        packed = []
        for b in group:
            for s in range(2):
                high, low = parts(buffer[s, b])
                gram = dot(high, jnp.concatenate([high, low], axis=1), ((0,), (0,))) * (1.0 / D)
                packed.append(packed_gram(gram[:, :BLOCK], gram[:, BLOCK:]))
        for k, b in enumerate(group):
            one, two = packed[2 * k : 2 * k + 2]
            for s, (quarters, diagonal) in enumerate((one, (one[0] + two[0], one[1] + two[1]))):
                if b < RIGHT - 1:
                    slots[2 * b + s, :BLOCK, :] = quarters
                    slots[2 * b + s, BLOCK : BLOCK + 1, :] = diagonal
                else:
                    slots[s * half : (s + 1) * half, BLOCK + 8 :, :] = quarters.reshape(half, SHARE, HALF)
                    for slot in range(ROWS):
                        slots[slot, BLOCK + 1 + s : BLOCK + 2 + s, :] = diagonal
        for b in group:
            if b < RIGHT - 1:
                pair = pl.ds(2 * b, 2)
                copies.append(pltpu.make_async_copy(slots.at[pair], out.at[pair], out_sems.at[b]))
                copies[-1].start()
    for copy in copies:
        copy.wait()


def left_stats_kernel(info, first, second, keep, send, buffer, sums, sems):
    core = info[0]
    tiles = fetched((first, second), buffer, sems)
    for b in range(RIGHT):
        for copy in tiles[b]:
            copy.wait()
        for s in range(2):
            for block in range(2):
                high, low = parts(buffer[s, b, block * BLOCK : (block + 1) * BLOCK, :])
                gram = dot(high, jnp.concatenate([high, low], axis=0), ((1,), (1,)))
                if b == 0:
                    sums[block, s] = gram
                else:
                    sums[block, s] += gram
    for out, block in ((keep, core), (send, 1 - core)):
        total = None
        for s in range(2):
            gram = sums[block, s] * (1.0 / FF)
            gram = packed_gram(gram[:, :BLOCK], gram[:, BLOCK:])
            total = gram if s == 0 else (total[0] + gram[0], total[1] + gram[1])
            out[s * PACK : s * PACK + BLOCK, :] = total[0]
            out[s * PACK + BLOCK : (s + 1) * PACK, :] = jnp.broadcast_to(total[1], (8, HALF))


def right_roots_kernel(arrived, right_out, diagonals):
    total = arrived[0]
    for slot in range(1, ROWS):
        total = total + arrived[slot]
    for slot in range(ROWS):
        right_out[slot, PACK:, :] = total[PACK:]
    diagonals[...] = total[BLOCK:PACK]
    (root,) = roots([unpacked(total[:PACK])])
    quarters, diagonal = packed_parts(root)
    for slot in range(ROWS):
        right_out[slot, :BLOCK, :] = quarters
        right_out[slot, BLOCK:PACK, :] = jnp.broadcast_to(diagonal, (8, HALF))


def left_root_kernel(own, other, out):
    (root,) = roots([unpacked(own[...] + other[...])])
    store_packed(out, 0, root)


def halfway_kernel(info, first, second, mine, other, out, buffer, results, sems, out_sems):
    core = info[0]
    tiles = fetched((first, second), buffer, sems)
    split = [[parts(unpacked(ref[s * PACK : (s + 1) * PACK, :])) for s in range(2)] for ref in (mine, other)]
    copies = []
    for b in range(RIGHT):
        for copy in tiles[b]:
            copy.wait()
        for s in range(2):
            for place, block in enumerate((core, 1 - core)):
                rows = pl.ds(pl.multiple_of(block * BLOCK, BLOCK), BLOCK)
                result = halves_product(split[place][s], parts(buffer[s, b, rows, :]))
                results[b, 2 * s, rows, :], results[b, 2 * s + 1, rows, :] = parts(result)
        copy = pltpu.make_async_copy(results.at[b], out.at[b], out_sems.at[b])
        copy.start()
        copies.append(copy)
    for copy in copies:
        copy.wait()


def applied(held, b, one, two, buffer):
    (h1, l1), (h2, l2) = one, two
    weights = jnp.concatenate([h1, h1, l1, h2, h2, l2], axis=0)
    for start in (0, BLOCK):
        rows = slice(start, start + BLOCK)
        high_one, low_one, high_two, low_two = [held[b, q, rows, :] for q in range(4)]
        lhs = jnp.concatenate([low_one, high_one, high_one, low_two, high_two, high_two], axis=1)
        buffer[b, rows, :] = dot(lhs, weights)
        yield


def finish_kernel(
    halfway, gathered, diagonals, out, held, buffer, sems, out_sems
):
    fetches = [pltpu.make_async_copy(halfway.at[b], held.at[b], sems.at[b]) for b in range(RIGHT)]
    for copy in fetches:
        copy.start()
    half = ROWS // 2
    statistics = [
        unpacked(gathered[s * half : (s + 1) * half, PACK:, :].reshape(BLOCK, HALF), diagonals[1 + s : 2 + s, :])
        for s in range(2)
    ]
    found = []
    chain = root_steps(statistics, found)
    copies = []

    def stored(b, start, size, sem):
        rows = pl.ds(start, size)
        copy = pltpu.make_async_copy(
            buffer.at[b, rows], out.at[rows, pl.ds(b * BLOCK, BLOCK)], out_sems.at[sem]
        )
        copy.start()
        copies.append(copy)

    for _ in range(8):
        next(chain)
    for copy in fetches:
        copy.wait()
    for b in range(RIGHT - 1):
        one, two = [parts(unpacked(gathered[2 * b + s, :PACK, :])) for s in range(2)]
        for _ in applied(held, b, one, two, buffer):
            next(chain, None)
        stored(b, 0, 2 * BLOCK, b)
    for _ in chain:
        pass
    last = RIGHT - 1
    for k, _ in enumerate(applied(held, last, parts(found[0]), parts(found[1]), buffer)):
        stored(last, k * BLOCK, BLOCK, last + k)
    for copy in copies:
        copy.wait()


VMEM = pl.BlockSpec(memory_space=pltpu.VMEM)
SMEM = pl.BlockSpec(memory_space=pltpu.SMEM)
HBM = pl.BlockSpec(memory_space=pltpu.HBM)


def in_hbm(*values):
    return [pltpu.with_memory_space_constraint(value, pltpu.HBM) for value in values]


def params():
    return pltpu.CompilerParams(vmem_limit_bytes=32 * 1024 * 1024)


def cost(flops, moved):
    return pl.CostEstimate(flops=int(flops), bytes_accessed=int(moved), transcendentals=0)


def body(grad_first, grad_second):
    rows, cols = grad_first.shape
    col = lax.axis_index("col")
    core = lax.rem(col, 2)
    low_y = lax.rem(col // 4, 2)
    info = core.reshape(1).astype(jnp.int32)
    pair = jax.ShapeDtypeStruct((2 * PACK, HALF), f32)
    single = jax.ShapeDtypeStruct((PACK, HALF), f32)
    grads = 2 * rows * cols * 4
    passes = 3 * 2 * BLOCK * rows * cols * 2
    newton = 20 * 6 * BLOCK**3
    tiles = [pltpu.VMEM((2, RIGHT, rows, BLOCK), f32)]
    tile_sems = [pltpu.SemaphoreType.DMA((2, RIGHT))]

    right_parts = pl.pallas_call(
        right_stats_kernel,
        in_specs=[HBM, HBM],
        out_specs=HBM,
        out_shape=pltpu.HBM((ROWS, SLOT, HALF), f32),
        scratch_shapes=tiles
        + [pltpu.VMEM((ROWS, SLOT, HALF), f32)]
        + tile_sems
        + [pltpu.SemaphoreType.DMA((RIGHT - 1,))],
        compiler_params=params(),
        cost_estimate=cost(passes, grads),
        name="right_stats",
    )(*in_hbm(grad_first, grad_second))
    arrived = exchanged(right_parts)

    info, right_parts = lax.optimization_barrier((info, right_parts))
    keep, send = pl.pallas_call(
        left_stats_kernel,
        in_specs=[SMEM, HBM, HBM],
        out_specs=[VMEM, VMEM],
        out_shape=[pair, pair],
        scratch_shapes=tiles + [pltpu.VMEM((2, 2, BLOCK, 2 * BLOCK), f32)] + tile_sems,
        compiler_params=params(),
        cost_estimate=cost(passes, grads),
        name="left_stats",
    )(info, *in_hbm(grad_first, grad_second))
    both = (keep + swap(send, 1)).reshape(2, PACK, HALF)
    own = lax.dynamic_index_in_dim(both, low_y, 0, keepdims=False)
    rest = lax.dynamic_index_in_dim(both, 1 - low_y, 0, keepdims=False)
    own = (own + swap(own, 8)) + (swap(rest, 4) + swap(rest, 12))
    left_in = [own, swap(own, 2)]
    own, arrived = lax.optimization_barrier((own, arrived))

    right_root, diagonals = pl.pallas_call(
        right_roots_kernel,
        in_specs=[VMEM],
        out_specs=[VMEM, VMEM],
        out_shape=[jax.ShapeDtypeStruct((ROWS, SLOT, HALF), f32), jax.ShapeDtypeStruct((8, HALF), f32)],
        compiler_params=params(),
        cost_estimate=cost(newton, 2 * ROWS * SLOT * HALF * 4),
        name="right_roots",
    )(arrived)
    left_in, right_root = lax.optimization_barrier((left_in, right_root))
    gathered = exchanged(right_root)
    left_in, right_root = lax.optimization_barrier((left_in, right_root))
    left_root = pl.pallas_call(
        left_root_kernel,
        in_specs=[VMEM, VMEM],
        out_specs=VMEM,
        out_shape=single,
        compiler_params=params(),
        cost_estimate=cost(newton, 3 * PACK * HALF * 4),
        name="left_root",
    )(*left_in)
    left_other = swap(left_root, 4)
    mine = jnp.where(
        low_y == 0,
        jnp.concatenate([left_root, left_other]),
        jnp.concatenate([left_other, left_root]),
    )
    other = swap(mine, 1)

    held = (RIGHT, 4, rows, BLOCK)
    tile_sem = pltpu.SemaphoreType.DMA((RIGHT,))
    halfway = pl.pallas_call(
        halfway_kernel,
        in_specs=[SMEM, HBM, HBM, VMEM, VMEM],
        out_specs=HBM,
        out_shape=pltpu.HBM(held, bf16),
        scratch_shapes=tiles + [pltpu.VMEM(held, bf16)] + tile_sems + [tile_sem],
        compiler_params=params(),
        cost_estimate=cost(passes, 2 * grads),
        name="halfway",
    )(info, *in_hbm(grad_first, grad_second), mine, other)

    return pl.pallas_call(
        finish_kernel,
        in_specs=[HBM, VMEM, VMEM],
        out_specs=HBM,
        scratch_shapes=[
            pltpu.VMEM(held, bf16),
            pltpu.VMEM((RIGHT, rows, BLOCK), f32),
            tile_sem,
            pltpu.SemaphoreType.DMA((RIGHT + 1,)),
        ],
        out_shape=jax.ShapeDtypeStruct((rows, cols), f32),
        compiler_params=params(),
        cost_estimate=cost(passes + 2 * newton, 2 * grads),
        name="finish",
    )(*in_hbm(halfway), gathered, diagonals)


def solution(mesh):
    in_specs = (P("row", "col"), P("row", "col"))
    out_specs = P("row", "col")
    return jax.shard_map(body, mesh=mesh, in_specs=in_specs, out_specs=out_specs, check_vma=False)
```

```python
import jax
import jax.numpy as jnp
from jax import lax
from jax.experimental import pallas as pl
from jax.experimental.pallas import tpu as pltpu
from jax.sharding import PartitionSpec as P

D = 4096
FF = 20480
BLOCK = 256
HALF = 128
ITERS = 6
DAMPING = 0.001
ROWS = 8
COLS = 16
RIGHT = 5
SHARE = 2 * BLOCK // ROWS
SLOT = BLOCK + 8 + SHARE
PACK = BLOCK + 8

f32 = jnp.float32
bf16 = jnp.bfloat16

def swap(value, d):
    return lax.ppermute(value, "col", [(i, i ^ d) for i in range(COLS)])


def exchanged(slots):
    return lax.all_to_all(slots, "row", split_axis=0, concat_axis=0, tiled=True)


def parts(value):
    high = value.astype(bf16)
    return high, (value - high.astype(f32)).astype(bf16)


def dot(left, right, dims=((1,), (0,))):
    return lax.dot_general(left, right, (dims, ((), ())), preferred_element_type=f32)


def product(left, right):
    (lh, ll), (rh, rl) = left, right
    return dot(lh, rh) + (dot(lh, rl) + dot(ll, rh))


def halves_product(left, right):
    return jnp.concatenate(
        [product([part[k : k + HALF] for part in left], right) for k in (0, HALF)], axis=0
    )


def iotas(n):
    return (
        lax.broadcasted_iota(jnp.int32, (n, n), 0),
        lax.broadcasted_iota(jnp.int32, (n, n), 1),
    )


def packed_parts(block):
    i, j = iotas(HALF)
    first, last = block[:HALF, :HALF], block[HALF:, HALF:]
    quarters = jnp.concatenate([block[:HALF, HALF:], jnp.where(i >= j, first, last)], axis=0)
    return quarters, jnp.sum(jnp.where(i == j, last, 0.0), axis=0, keepdims=True)


def packed_gram(even, odd):
    i, j = iotas(HALF)
    first, last = odd[:HALF, :HALF], odd[HALF:, HALF:]
    upper = even[:HALF, HALF:] + odd[:HALF, HALF:] + odd[HALF:, :HALF].T
    mixed = jnp.where(i >= j, even[:HALF, :HALF] + first, even[HALF:, HALF:] + last)
    mixed = mixed + jnp.where(i <= j, first, last).T
    diagonal = jnp.sum(jnp.where(i == j, even[HALF:, HALF:] + 2.0 * last, 0.0), axis=0, keepdims=True)
    return jnp.concatenate([upper, mixed], axis=0), diagonal


def store_packed(ref, start, block):
    quarters, diagonal = packed_parts(block)
    ref[pl.ds(start, BLOCK), :] = quarters
    ref[pl.ds(start + BLOCK, 8), :] = jnp.broadcast_to(diagonal, (8, HALF))


def unpacked(packed, diagonal=None):
    i, j = iotas(HALF)
    upper, mixed = packed[:HALF], packed[HALF:BLOCK]
    if diagonal is None:
        diagonal = packed[BLOCK : BLOCK + 1]
    turned = mixed.T
    first = jnp.where(i >= j, mixed, turned)
    last = jnp.where(i < j, mixed, jnp.where(i == j, jnp.broadcast_to(diagonal, (HALF, HALF)), turned))
    return jnp.concatenate(
        [
            jnp.concatenate([first, upper], axis=1),
            jnp.concatenate([upper.T, last], axis=1),
        ],
        axis=0,
    )


def root_steps(statistics, found):
    i, j = iotas(BLOCK)
    identity = jnp.where(i == j, 1.0, 0.0).astype(f32)
    currents, scaleds, squares = [], [], []
    for statistic in statistics:
        damped = statistic + DAMPING * identity
        split = parts(damped)
        square = halves_product(split, split)
        norm = jnp.sqrt(jnp.sum(damped * damped, axis=(0, 1), keepdims=True))
        inverse = 1.0 / norm
        scaled = damped * inverse
        currents.append(lax.rsqrt(jnp.sqrt(norm)))
        scaleds.append(scaled)
        squares.append(
            parts((25.0 / 16.0) * identity - (10.0 / 16.0) * scaled + (square * inverse) * (inverse * (1.0 / 16.0)))
        )
    yield
    for iteration in range(ITERS):
        factors = [(5.0 * identity - scaled) * 0.25 for scaled in scaleds]
        split = [parts(factor) for factor in factors]
        if iteration == ITERS - 1:
            found.extend(halves_product(parts(current), fs) for current, fs in zip(currents, split))
            return
        if iteration == 0:
            currents = [current * factor for current, factor in zip(currents, factors)]
        else:
            squares = [parts(halves_product(fs, fs)) for fs in split]
            yield
            currents = [halves_product(parts(current), fs) for current, fs in zip(currents, split)]
        fourths = [parts(halves_product(sq, sq)) for sq in squares]
        yield
        scaleds = [halves_product(fo, parts(scaled)) for fo, scaled in zip(fourths, scaleds)]
        yield


def roots(statistics):
    found = []
    for _ in root_steps(statistics, found):
        pass
    return found


def fetched(sources, buffer, sems, order=range(RIGHT)):
    tiles = {}
    for b in order:
        columns = pl.ds(b * BLOCK, BLOCK)
        tiles[b] = [
            pltpu.make_async_copy(source.at[:, columns], buffer.at[s, b], sems.at[s, b])
            for s, source in enumerate(sources)
        ]
        for copy in tiles[b]:
            copy.start()
    return tiles


def right_stats_kernel(first, second, out, buffer, slots, sems, out_sems):
    groups = ((RIGHT - 1,), (0, 1), (2, 3))
    tiles = fetched((first, second), buffer, sems, sum(groups, ()))
    half = ROWS // 2
    copies = []
    for slot in range(ROWS):
        slots[slot, BLOCK + 3 : BLOCK + 8, :] = jnp.zeros((5, HALF), f32)
    for group in groups:
        for b in group:
            for copy in tiles[b]:
                copy.wait()
        packed = []
        for b in group:
            for s in range(2):
                high, low = parts(buffer[s, b])
                gram = dot(high, jnp.concatenate([high, low], axis=1), ((0,), (0,))) * (1.0 / D)
                packed.append(packed_gram(gram[:, :BLOCK], gram[:, BLOCK:]))
        for k, b in enumerate(group):
            one, two = packed[2 * k : 2 * k + 2]
            for s, (quarters, diagonal) in enumerate((one, (one[0] + two[0], one[1] + two[1]))):
                if b < RIGHT - 1:
                    slots[2 * b + s, :BLOCK, :] = quarters
                    slots[2 * b + s, BLOCK : BLOCK + 1, :] = diagonal
                else:
                    slots[s * half : (s + 1) * half, BLOCK + 8 :, :] = quarters.reshape(half, SHARE, HALF)
                    for slot in range(ROWS):
                        slots[slot, BLOCK + 1 + s : BLOCK + 2 + s, :] = diagonal
        for b in group:
            if b < RIGHT - 1:
                pair = pl.ds(2 * b, 2)
                copies.append(pltpu.make_async_copy(slots.at[pair], out.at[pair], out_sems.at[b]))
                copies[-1].start()
    for copy in copies:
        copy.wait()


def left_stats_kernel(info, first, second, keep, send, buffer, sums, sems):
    core = info[0]
    tiles = fetched((first, second), buffer, sems)
    for b in range(RIGHT):
        for copy in tiles[b]:
            copy.wait()
        for s in range(2):
            for block in range(2):
                high, low = parts(buffer[s, b, block * BLOCK : (block + 1) * BLOCK, :])
                gram = dot(high, jnp.concatenate([high, low], axis=0), ((1,), (1,)))
                if b == 0:
                    sums[block, s] = gram
                else:
                    sums[block, s] += gram
    for out, block in ((keep, core), (send, 1 - core)):
        total = None
        for s in range(2):
            gram = sums[block, s] * (1.0 / FF)
            gram = packed_gram(gram[:, :BLOCK], gram[:, BLOCK:])
            total = gram if s == 0 else (total[0] + gram[0], total[1] + gram[1])
            out[s * PACK : s * PACK + BLOCK, :] = total[0]
            out[s * PACK + BLOCK : (s + 1) * PACK, :] = jnp.broadcast_to(total[1], (8, HALF))


def right_roots_kernel(arrived, right_out, diagonals):
    total = arrived[0]
    for slot in range(1, ROWS):
        total = total + arrived[slot]
    for slot in range(ROWS):
        right_out[slot, PACK:, :] = total[PACK:]
    diagonals[...] = total[BLOCK:PACK]
    (root,) = roots([unpacked(total[:PACK])])
    quarters, diagonal = packed_parts(root)
    for slot in range(ROWS):
        right_out[slot, :BLOCK, :] = quarters
        right_out[slot, BLOCK:PACK, :] = jnp.broadcast_to(diagonal, (8, HALF))


def left_root_kernel(own, other, out):
    (root,) = roots([unpacked(own[...] + other[...])])
    store_packed(out, 0, root)


def halfway_kernel(info, first, second, mine, other, out, buffer, results, sems, out_sems):
    core = info[0]
    tiles = fetched((first, second), buffer, sems)
    split = [[parts(unpacked(ref[s * PACK : (s + 1) * PACK, :])) for s in range(2)] for ref in (mine, other)]
    copies = []
    for b in range(RIGHT):
        for copy in tiles[b]:
            copy.wait()
        for s in range(2):
            for place, block in enumerate((core, 1 - core)):
                rows = pl.ds(pl.multiple_of(block * BLOCK, BLOCK), BLOCK)
                result = halves_product(split[place][s], parts(buffer[s, b, rows, :]))
                results[b, 2 * s, rows, :], results[b, 2 * s + 1, rows, :] = parts(result)
        copy = pltpu.make_async_copy(results.at[b], out.at[b], out_sems.at[b])
        copy.start()
        copies.append(copy)
    for copy in copies:
        copy.wait()


def applied(held, b, one, two, buffer):
    (h1, l1), (h2, l2) = one, two
    weights = jnp.concatenate([h1, h1, l1, h2, h2, l2], axis=0)
    for start in (0, BLOCK):
        rows = slice(start, start + BLOCK)
        high_one, low_one, high_two, low_two = [held[b, q, rows, :] for q in range(4)]
        lhs = jnp.concatenate([low_one, high_one, high_one, low_two, high_two, high_two], axis=1)
        buffer[b, rows, :] = dot(lhs, weights)
        yield


def finish_kernel(
    halfway, gathered, diagonals, out, held, buffer, sems, out_sems
):
    fetches = [pltpu.make_async_copy(halfway.at[b], held.at[b], sems.at[b]) for b in range(RIGHT)]
    for copy in fetches:
        copy.start()
    half = ROWS // 2
    statistics = [
        unpacked(gathered[s * half : (s + 1) * half, PACK:, :].reshape(BLOCK, HALF), diagonals[1 + s : 2 + s, :])
        for s in range(2)
    ]
    found = []
    chain = root_steps(statistics, found)
    copies = []

    def stored(b, start, size, sem):
        rows = pl.ds(start, size)
        copy = pltpu.make_async_copy(
            buffer.at[b, rows], out.at[rows, pl.ds(b * BLOCK, BLOCK)], out_sems.at[sem]
        )
        copy.start()
        copies.append(copy)

    for _ in range(9):
        next(chain)
    for copy in fetches:
        copy.wait()
    for b in range(RIGHT - 1):
        one, two = [parts(unpacked(gathered[2 * b + s, :PACK, :])) for s in range(2)]
        for _ in applied(held, b, one, two, buffer):
            next(chain, None)
        stored(b, 0, 2 * BLOCK, b)
    for _ in chain:
        pass
    last = RIGHT - 1
    for k, _ in enumerate(applied(held, last, parts(found[0]), parts(found[1]), buffer)):
        stored(last, k * BLOCK, BLOCK, last + k)
    for copy in copies:
        copy.wait()


VMEM = pl.BlockSpec(memory_space=pltpu.VMEM)
SMEM = pl.BlockSpec(memory_space=pltpu.SMEM)
HBM = pl.BlockSpec(memory_space=pltpu.HBM)


def in_hbm(*values):
    return [pltpu.with_memory_space_constraint(value, pltpu.HBM) for value in values]


def params():
    return pltpu.CompilerParams(vmem_limit_bytes=32 * 1024 * 1024)


def cost(flops, moved):
    return pl.CostEstimate(flops=int(flops), bytes_accessed=int(moved), transcendentals=0)


def body(grad_first, grad_second):
    rows, cols = grad_first.shape
    col = lax.axis_index("col")
    core = lax.rem(col, 2)
    low_y = lax.rem(col // 4, 2)
    info = core.reshape(1).astype(jnp.int32)
    pair = jax.ShapeDtypeStruct((2 * PACK, HALF), f32)
    single = jax.ShapeDtypeStruct((PACK, HALF), f32)
    grads = 2 * rows * cols * 4
    passes = 3 * 2 * BLOCK * rows * cols * 2
    newton = 20 * 6 * BLOCK**3
    tiles = [pltpu.VMEM((2, RIGHT, rows, BLOCK), f32)]
    tile_sems = [pltpu.SemaphoreType.DMA((2, RIGHT))]

    right_parts = pl.pallas_call(
        right_stats_kernel,
        in_specs=[HBM, HBM],
        out_specs=HBM,
        out_shape=pltpu.HBM((ROWS, SLOT, HALF), f32),
        scratch_shapes=tiles
        + [pltpu.VMEM((ROWS, SLOT, HALF), f32)]
        + tile_sems
        + [pltpu.SemaphoreType.DMA((RIGHT - 1,))],
        compiler_params=params(),
        cost_estimate=cost(passes, grads),
        name="right_stats",
    )(*in_hbm(grad_first, grad_second))
    arrived = exchanged(right_parts)

    info, right_parts = lax.optimization_barrier((info, right_parts))
    keep, send = pl.pallas_call(
        left_stats_kernel,
        in_specs=[SMEM, HBM, HBM],
        out_specs=[VMEM, VMEM],
        out_shape=[pair, pair],
        scratch_shapes=tiles + [pltpu.VMEM((2, 2, BLOCK, 2 * BLOCK), f32)] + tile_sems,
        compiler_params=params(),
        cost_estimate=cost(passes, grads),
        name="left_stats",
    )(info, *in_hbm(grad_first, grad_second))
    both = (keep + swap(send, 1)).reshape(2, PACK, HALF)
    own = lax.dynamic_index_in_dim(both, low_y, 0, keepdims=False)
    rest = lax.dynamic_index_in_dim(both, 1 - low_y, 0, keepdims=False)
    own = (own + swap(own, 8)) + (swap(rest, 4) + swap(rest, 12))
    left_in = [own, swap(own, 2)]
    own, arrived = lax.optimization_barrier((own, arrived))

    right_root, diagonals = pl.pallas_call(
        right_roots_kernel,
        in_specs=[VMEM],
        out_specs=[VMEM, VMEM],
        out_shape=[jax.ShapeDtypeStruct((ROWS, SLOT, HALF), f32), jax.ShapeDtypeStruct((8, HALF), f32)],
        compiler_params=params(),
        cost_estimate=cost(newton, 2 * ROWS * SLOT * HALF * 4),
        name="right_roots",
    )(arrived)
    left_in, right_root = lax.optimization_barrier((left_in, right_root))
    gathered = exchanged(right_root)
    left_in, right_root = lax.optimization_barrier((left_in, right_root))
    left_root = pl.pallas_call(
        left_root_kernel,
        in_specs=[VMEM, VMEM],
        out_specs=VMEM,
        out_shape=single,
        compiler_params=params(),
        cost_estimate=cost(newton, 3 * PACK * HALF * 4),
        name="left_root",
    )(*left_in)
    left_other = swap(left_root, 4)
    mine = jnp.where(
        low_y == 0,
        jnp.concatenate([left_root, left_other]),
        jnp.concatenate([left_other, left_root]),
    )
    other = swap(mine, 1)

    held = (RIGHT, 4, rows, BLOCK)
    tile_sem = pltpu.SemaphoreType.DMA((RIGHT,))
    halfway = pl.pallas_call(
        halfway_kernel,
        in_specs=[SMEM, HBM, HBM, VMEM, VMEM],
        out_specs=HBM,
        out_shape=pltpu.HBM(held, bf16),
        scratch_shapes=tiles + [pltpu.VMEM(held, bf16)] + tile_sems + [tile_sem],
        compiler_params=params(),
        cost_estimate=cost(passes, 2 * grads),
        name="halfway",
    )(info, *in_hbm(grad_first, grad_second), mine, other)

    return pl.pallas_call(
        finish_kernel,
        in_specs=[HBM, VMEM, VMEM],
        out_specs=HBM,
        scratch_shapes=[
            pltpu.VMEM(held, bf16),
            pltpu.VMEM((RIGHT, rows, BLOCK), f32),
            tile_sem,
            pltpu.SemaphoreType.DMA((RIGHT + 1,)),
        ],
        out_shape=jax.ShapeDtypeStruct((rows, cols), f32),
        compiler_params=params(),
        cost_estimate=cost(passes + 2 * newton, 2 * grads),
        name="finish",
    )(*in_hbm(halfway), gathered, diagonals)


def solution(mesh):
    in_specs = (P("row", "col"), P("row", "col"))
    out_specs = P("row", "col")
    return jax.shard_map(body, mesh=mesh, in_specs=in_specs, out_specs=out_specs, check_vma=False)
```
